512 devices in a mesh: src: 8 (over x, y_lo), feat: 64 (over y_hi, z, core).
Axes of the slice: x: 4, y: 4 (y_hi: 2, y_lo: 2; y = y_hi * 2 + y_lo), z: 16, core: 2. Of those that a mesh axis runs over, the one named last changes fastest.
Arguments:
- residual: bfloat16 [448, 2304], P(None, 'src'), may hold values from -80 to 80
- token_ids: int32 [448], replicated, may hold values from 0 to 255999, as said below
- ffn_gain: bfloat16 [2304], P('src'), may hold values from 0.25 to 1.75
- gate_w: bfloat16 [2304, 18432], P('src', 'feat'), may hold values from -0.125 to 0.125
- up_w: bfloat16 [2304, 18432], P('src', 'feat'), may hold values from -0.125 to 0.125
- down_w: bfloat16 [18432, 2304], P('feat', 'src'), may hold values from -0.046875 to 0.046875
- enc_w: bfloat16 [2304, 65536], P(None, ('src', 'feat')), may hold values from -0.41666667 to 0.41666667
- enc_bias: bfloat16 [65536], P(('src', 'feat')), may hold values from -1 to 0.5
- dec_w: bfloat16 [65536, 2304], P(('src', 'feat')), may hold values from -0.0390625 to 0.0390625
- dec_bias: bfloat16 [2304], replicated, may hold values from -3 to 3
- enc_first: bfloat16 [2304, 65536], P(None, ('src', 'feat')), may hold values from -0.00010347366 to 0.00010347366
- enc_second: bfloat16 [2304, 65536], P(None, ('src', 'feat')), may hold values from 3.3105607e-10 to 3.3032848e-09
- dec_first: bfloat16 [65536, 2304], P(('src', 'feat')), may hold values from -0.00010347366 to 0.00010347366
- dec_second: bfloat16 [65536, 2304], P(('src', 'feat')), may hold values from 3.3105607e-10 to 3.3032848e-09
Outputs:
- enc_update: bfloat16 [2304, 65536], P(None, ('src', 'feat'))
- dec_update: bfloat16 [65536, 2304], P(('src', 'feat'))
The draws below stay inside these ranges and needn't reach their ends.
Inputs may be any that keep to these rules, and one draw needn't show every extreme that they name: `token_ids`: token ids of the batch; ids under 4 are control tokens.
All inputs are finite; a program needn't handle non-finite values.
Results may differ from the reference program's by a relative error of at most 0.01.
Values may be sent and summed in bfloat16 or wider, within the bound.
A program may use at most 128 MiB of HBM per device.

```python
import math
import jax
import jax.numpy as jnp
from jax import lax

D = 2304
FF = 18432
VOCAB = 256000
SPECIAL = 4
TOK = 448
SAE_F = 65536


def draw_token_ids(key, part):
    key = jax.random.fold_in(key, 7)
    key_kind, key_low, key_high = jax.random.split(key, 3)
    kinds = jax.random.randint(key_kind, (TOK,), 0, 4)
    low_ids = jax.random.randint(key_low, (TOK,), 0, SPECIAL)
    high_ids = jax.random.randint(key_high, (TOK,), SPECIAL, VOCAB)
    return jnp.where(kinds == 0, low_ids, high_ids).astype(jnp.int32)


def geometric_ramp(count, low, high):
    position = jnp.arange(count, dtype=jnp.float32) / float(count - 1)
    return low * jnp.exp(jnp.log(high / low) * position)


def draw_residual(key, part):
    key = jax.random.fold_in(key, 17)
    key_vals, key_perm = jax.random.split(key)
    values = jnp.clip(jax.random.normal(key_vals, (TOK, D), jnp.float32), -4.0, 4.0)
    columns = geometric_ramp(D, 0.4, 2.4)
    rows = geometric_ramp(TOK, 0.3, 3.0)
    rows = jax.random.permutation(key_perm, rows)
    return (values * rows[:, None] * columns[None, :]).astype(jnp.bfloat16)


def feature_scales(ratio):
    position = jnp.arange(SAE_F, dtype=jnp.float32) / float(SAE_F - 1)
    return jnp.exp(jnp.log(ratio) * position)


def draw_enc_w(key, part):
    key = jax.random.fold_in(key, 11)
    scales = feature_scales(3.0)
    values = jnp.clip(jax.random.normal(key, (D, SAE_F), jnp.float32), -4.0, 4.0)
    return (values * D ** (-0.5) * scales[None, :]).astype(jnp.bfloat16)


def draw_dec_w(key, part):
    key = jax.random.fold_in(key, 13)
    scales = feature_scales(3.0)
    values = jnp.clip(jax.random.normal(key, (SAE_F, D), jnp.float32), -4.0, 4.0)
    return (values * 0.5 * SAE_F ** (-0.5) * scales[:, None]).astype(jnp.bfloat16)


def block_scale(own_key, shape, cuts, low, high):
    gain = 1.0
    for axis_at, shards_of in cuts:
        draws = jax.random.uniform(jax.random.fold_in(jax.random.fold_in(own_key, 6), axis_at), (shards_of,), jnp.float32, low / len(cuts), high / len(cuts))
        gain = gain * jnp.repeat(jnp.exp(draws), shape[axis_at] // shards_of).reshape((-1,) + (1,) * (len(shape) - 1 - axis_at))
    return gain


def normal_values(key, shape, scale, most, shards=(), kind=jnp.bfloat16):
    values = scale * jax.random.normal(key, shape, jnp.float32)
    if shards:
        values = values * block_scale(key, shape, shards, -0.22, 0.18)
    return jnp.clip(values, -most, most).astype(kind)


def setup_inputs(seed: int = 0) -> dict:
    splits = jax.random.split(jax.random.key(seed), 15)
    return {
        "residual": draw_residual(jax.random.fold_in(splits[14], 71), 0),
        "token_ids": draw_token_ids(jax.random.fold_in(splits[14], 71), 0),
        "ffn_gain": jnp.clip(1.0 + 0.15 * jax.random.normal(splits[2], (D,), jnp.float32), 0.25, 1.75).astype(jnp.bfloat16),
        "gate_w": normal_values(splits[3], (D, FF), D ** -0.5, 0.125, ((0, 8), (1, 64))),
        "up_w": normal_values(splits[4], (D, FF), D ** -0.5, 0.125, ((0, 8), (1, 64))),
        "down_w": normal_values(splits[5], (FF, D), FF ** -0.5, 0.046875, ((0, 64), (1, 8))),
        "enc_w": draw_enc_w(jax.random.fold_in(splits[14], 71), 0),
        "enc_bias": jnp.clip(-1.0 + 1.5 * jax.random.uniform(splits[7], (SAE_F,), jnp.float32) ** block_scale(splits[7], (SAE_F,), ((0, 512),), -0.2, 0.2), -1.0, 0.5).astype(jnp.bfloat16),
        "dec_w": draw_dec_w(jax.random.fold_in(splits[14], 71), 0),
        "dec_bias": normal_values(splits[9], (D,), 0.5, 3.0),
        "enc_first": normal_values(splits[10], (D, SAE_F), (0.3 * (2 * D * SAE_F) ** -0.5), 0.00010347366, ((1, 512),)),
        "enc_second": jnp.clip(jnp.exp(math.log(3.3032847568392754e-09) - 2.30038487 * jax.random.uniform(splits[11], (D, SAE_F), jnp.float32) ** block_scale(splits[11], (D, SAE_F), ((1, 512),), -0.2, 0.2)), 3.310560714453459e-10, 3.3032847568392754e-09).astype(jnp.bfloat16),
        "dec_first": normal_values(splits[12], (SAE_F, D), (0.3 * (2 * D * SAE_F) ** -0.5), 0.00010347366, ((0, 512),)),
        "dec_second": jnp.clip(jnp.exp(math.log(3.3032847568392754e-09) - 2.30038487 * jax.random.uniform(splits[13], (SAE_F, D), jnp.float32) ** block_scale(splits[13], (SAE_F, D), ((0, 512),), -0.2, 0.2)), 3.310560714453459e-10, 3.3032847568392754e-09).astype(jnp.bfloat16),
    }


eps_rms = 1e-06
beta_one = 0.9
beta_two = 0.999
adam_count = 100.0
l1_coeff = 0.2

def adam_direction(grad, first, second, clip_factor):
    scaled_grad = clip_factor * grad
    first_new = beta_one * first.astype(jnp.float32) + (1.0 - beta_one) * scaled_grad
    second_new = beta_two * second.astype(jnp.float32) + (1.0 - beta_two) * scaled_grad * scaled_grad
    corr_one = 1.0 - beta_one ** adam_count
    corr_two = 1.0 - beta_two ** adam_count
    return (first_new / corr_one / (jnp.sqrt(second_new / corr_two) + 1e-08)).astype(jnp.bfloat16)

def reference(residual, token_ids, ffn_gain, gate_w, up_w, down_w, enc_w, enc_bias, dec_w, dec_bias, enc_first, enc_second, dec_first, dec_second):
    res_float = residual.astype(jnp.float32)
    inverse_rms = lax.rsqrt(lax.optimization_barrier(jnp.mean(res_float * res_float, axis=1, keepdims=True)) + eps_rms)
    normed = (res_float * inverse_rms * ffn_gain.astype(jnp.float32)).astype(jnp.bfloat16)
    gate_acts = jnp.dot(normed, gate_w, preferred_element_type=jnp.float32)
    up_acts = jnp.dot(normed, up_w, preferred_element_type=jnp.float32)
    hidden = (jax.nn.gelu(gate_acts, approximate=True) * up_acts).astype(jnp.bfloat16)
    stream = (res_float + jnp.dot(hidden, down_w, preferred_element_type=jnp.float32)).astype(jnp.bfloat16)
    stream_float = stream.astype(jnp.float32)
    scaled = (stream_float * lax.rsqrt(lax.optimization_barrier(jnp.mean(stream_float * stream_float, axis=1, keepdims=True)) + eps_rms)).astype(jnp.bfloat16)
    pre_acts = jnp.dot(scaled, enc_w, preferred_element_type=jnp.float32) + enc_bias.astype(jnp.float32)
    latents = jnp.maximum(pre_acts, 0.0).astype(jnp.bfloat16)
    recon = jnp.dot(latents, dec_w, preferred_element_type=jnp.float32)
    errors = (recon + dec_bias.astype(jnp.float32) - scaled.astype(jnp.float32)).astype(jnp.bfloat16)
    live_mask = (token_ids >= SPECIAL).astype(jnp.float32)
    token_weight = live_mask / jnp.maximum(jnp.sum(live_mask), 1.0)
    err_grad = (2.0 * token_weight[:, None] * errors.astype(jnp.float32)).astype(jnp.bfloat16)
    dec_grad = jnp.dot(latents.T, err_grad, preferred_element_type=jnp.float32)
    lat_grad = jnp.dot(err_grad, dec_w.T, preferred_element_type=jnp.float32) + l1_coeff * token_weight[:, None]
    pre_grad = jnp.where(pre_acts > 0.0, lat_grad, jnp.zeros_like(lat_grad)).astype(jnp.bfloat16)
    enc_grad = jnp.dot(scaled.T, pre_grad, preferred_element_type=jnp.float32)
    grad_total = jnp.sum(enc_grad * enc_grad) + jnp.sum(dec_grad * dec_grad)
    clip_factor = lax.rsqrt(grad_total + 1e-12)
    enc_update = adam_direction(enc_grad, enc_first, enc_second, clip_factor)
    dec_update = adam_direction(dec_grad, dec_first, dec_second, clip_factor)
    return (enc_update, dec_update)
```

```python
import functools

import jax
import jax.numpy as jnp
from jax import lax
from jax.experimental import pallas as pl
from jax.experimental.pallas import tpu as pltpu
from jax.sharding import PartitionSpec as P

SPECIAL = 4
TOK = 448
HALF = 224
D = 2304
W = 288
ZN = 16
SRC = 8
FEAT = 64

eps_rms = 1e-06
beta_one = 0.9
beta_two = 0.999
adam_count = 100.0
l1_coeff = 0.2

F32 = jnp.float32
BF16 = jnp.bfloat16


def tiles(v):
    return v.reshape(v.shape[0] // 16, 16, 128)


def rows(v):
    return v.reshape(v.shape[0] * 16, 128)


def dot(a, b, ca=1, cb=0):
    return lax.dot_general(a, b, (((ca,), (cb,)), ((), ())), preferred_element_type=F32)


def lane_group(shape):
    return lax.broadcasted_iota(jnp.int32, shape, len(shape) - 1)


def fold(read, lanes):
    out = read(3)
    for g in (2, 1, 0):
        out = jnp.where(lanes < 32 * (g + 1), read(g), out)
    return out


def adam(grad, first, second, clip):
    scaled_grad = clip * grad
    first_new = beta_one * first.astype(F32) + (1.0 - beta_one) * scaled_grad
    second_new = beta_two * second.astype(F32) + (1.0 - beta_two) * scaled_grad * scaled_grad
    corr_one = 1.0 - beta_one**adam_count
    corr_two = 1.0 - beta_two**adam_count
    return (first_new / corr_one / (jnp.sqrt(second_new / corr_two) + 1e-08)).astype(BF16)


def kernel(
    res, tok, gain, gw, uw, dw_h, ew_h, eb, dcw_h, db, ef_h, es_h, df_h, ds_h,
    eo, do,
    dw, ew, dcw, ef, es, df, ds, ebx,
    rn, rt, gu, p1r, sqs, sqr, hb, hh, dwf, tail, rest, ot, p3r,
    gs, ss, twb, bias, pa, lat_t, tt, p5r, aa, p5z, ee, st,
    dg, dgs, dgr, eg, egs, egr, n7, n7z, n7x, n7c,
    lsem, wsend, wrecv, ssem, rsem,
):
    s = lax.axis_index("src")
    f = lax.axis_index("feat")
    c = lax.rem(f, 2)
    q = lax.div(f, 2)
    z = lax.rem(q, ZN)
    yhi = lax.div(q, ZN)
    xy = s * 2 + yhi
    half = lax.div(s, 4)

    def to(src, feat):
        return {"device_id": (src, feat), "device_id_type": pl.DeviceIdType.MESH}

    other = to(s, q * 2 + 1 - c)

    def src_peer(d, core):
        return to(lax.rem(s + d, SRC), q * 2 + core)

    def q_peer(d):
        return to(s, lax.rem(q + d, 32) * 2 + c)

    def z_peer(d):
        return to(s, (yhi * ZN + lax.rem(z + d, ZN)) * 2 + c)

    def xy_peer(d):
        i = lax.rem(xy + d, 16)
        return to(lax.div(i, 2), (lax.rem(i, 2) * ZN + z) * 2 + c)

    def loop(n, fn):
        def body(d, carry):
            fn(d)
            return carry

        lax.fori_loop(1, n, body, 0)

    def send(src, dst, k, where):
        pltpu.make_async_remote_copy(
            src_ref=src, dst_ref=dst, send_sem=ssem.at[k], recv_sem=rsem.at[k], **where
        ).start()

    def arrived(ref, k):
        pltpu.make_async_copy(ref, ref, rsem.at[k]).wait()

    def left(ref, k):
        pltpu.make_async_copy(ref, ref, ssem.at[k]).wait()

    barrier = pltpu.get_barrier_semaphore()
    pl.semaphore_signal(barrier, inc=1, **other)

    def greet(d):
        pl.semaphore_signal(barrier, inc=1, **src_peer(d, c))
        pl.semaphore_signal(barrier, inc=1, **src_peer(d, 1 - c))
        pl.semaphore_signal(
            barrier, inc=1, **to(lax.rem(s + d, SRC), (lax.rem(yhi + 1, 2) * ZN + z) * 2 + c)
        )

    loop(SRC, greet)
    loop(32, lambda d: pl.semaphore_signal(barrier, inc=1, **q_peer(d)))

    loads = []
    for k, (src, dst) in enumerate(
        ((dw_h, dw), (ew_h, ew.at[0]), (dcw_h, dcw.at[0]), (ef_h, ef), (es_h, es), (df_h, df), (ds_h, ds))
    ):
        cp = pltpu.make_async_copy(src, dst, lsem.at[k])
        cp.start()
        loads.append(cp)

    lanes = lane_group((64, 128))
    wide = lane_group((128, 128))
    pick = jnp.where(
        jnp.bitwise_and(lane_group((32, 128)), 31) == lax.broadcasted_iota(jnp.int32, (32, 128), 0), 1.0, 0.0
    ).astype(BF16)

    resf = res[...].astype(F32)
    xg = (resf * gain[...].astype(F32)).astype(BF16)
    for k, w in enumerate((gw, uw)):
        main = dot(xg, w[:, 0:256])
        spread = dot(w[:, 256:288], pick).astype(BF16)
        tail[0:448] = dot(xg, spread)
        tail[448:512] = jnp.zeros((64, 128), F32)
        for h in range(2):
            for j in range(2):
                gu[k, h * 32 + 14 * j : h * 32 + 14 * j + 14] = tiles(
                    main[224 * h : 224 * h + 224, 128 * j : 128 * j + 128].astype(BF16)
                )
            part = fold(lambda g: tail[224 * h + 64 * g : 224 * h + 64 * g + 64], lanes)
            gu[k, h * 32 + 28 : h * 32 + 32] = tiles(part.astype(BF16))
    squares = jnp.sum(resf * resf, axis=1, keepdims=True)
    squares = jnp.concatenate([squares, jnp.zeros((64, 1), F32)], axis=0)
    cols = jnp.zeros((128, 128), F32)
    for k in range(4):
        cols = jnp.where(wide == k, squares[128 * k : 128 * k + 128], cols)
    sqs[...] = cols.T[0:8]

    pl.semaphore_wait(barrier, 53)

    def send_p1(d):
        t = lax.rem(s + d, SRC)
        send(gu.at[:, pl.ds(8 * t, 8)], p1r.at[d - 1], 0, src_peer(d, c))
        send(sqs, sqr.at[d - 1], 1, src_peer(d, c))

    loop(SRC, send_p1)

    ids = tok[...]
    live = jnp.where(ids >= SPECIAL, 1.0, 0.0)
    weight = live / jnp.maximum(jnp.sum(live), 1.0)
    weight = jnp.concatenate([weight, jnp.zeros((1, 64), F32)], axis=1)
    weight = jnp.concatenate(
        [weight[:, 128 * k : 128 * k + 128] for k in range(4)] + [jnp.zeros((124, 128), F32)], axis=0
    ).T
    for k in range(4):
        twb[128 * k : 128 * k + 128] = jnp.broadcast_to(weight[:, k : k + 1], (128, 128))
    for k in range(18):
        bias[k] = jnp.broadcast_to(db[:, 128 * k : 128 * k + 128].astype(F32), (8, 128))
    ebx[0] = jnp.broadcast_to(eb[...].astype(F32), (8, 128))

    def share(ref, k):
        return pltpu.make_async_remote_copy(
            src_ref=ref.at[0], dst_ref=ref.at[1], send_sem=wsend.at[k], recv_sem=wrecv.at[k], **other
        )

    shares = [share(ebx, 0), share(dwf, 1), share(ew, 2), share(dcw, 3)]
    shares[0].start()
    loads[0].wait()
    spread = dot(dw[:, 256:288], pick).astype(BF16)
    dwf[0, 0:256, 0:256] = dw[0:256, 0:256]
    dwf[0, 0:256, 256:384] = spread[0:256]
    for g in range(4):
        dwf[0, 256 + 32 * g : 288 + 32 * g, 0:256] = dw[256:288, 0:256]
        dwf[0, 256 + 32 * g : 288 + 32 * g, 256:384] = spread[256:288]
    shares[1].start()
    loads[1].wait()
    shares[2].start()
    loads[2].wait()
    shares[3].start()

    off = pl.multiple_of(HALF * c, 32)
    for j in range(2):
        rest[14 * j : 14 * j + 14] = tiles(res[pl.ds(off, HALF), 128 * j : 128 * j + 128].astype(F32))
    tail[0:448] = dot(res[:, 256:288], pick)
    tail[448:512] = jnp.zeros((64, 128), F32)
    rest[28:32] = tiles(fold(lambda g: tail[pl.ds(off + 64 * g, 64)], lanes))
    ss[252:256] = jnp.zeros((4, 16, 128), BF16)
    tt[252:256] = jnp.zeros((4, 16, 128), BF16)

    arrived(sqr, 1)
    total = sqs[...]
    for d in range(7):
        total = total + sqr[d]
    inv = lax.rsqrt(total / D + eps_rms)
    inv = jnp.concatenate([inv, jnp.zeros((120, 128), F32)], axis=0).T
    for k in range(4):
        rn[128 * k : 128 * k + 128] = jnp.broadcast_to(inv[:, k : k + 1], (128, 128))
    for h in range(2):
        for j in range(2):
            rt[h * 32 + 14 * j : h * 32 + 14 * j + 14] = tiles(rn[224 * h : 224 * h + 224])
        rt[h * 32 + 28 : h * 32 + 32] = tiles(
            fold(lambda g: rn[224 * h + 64 * g : 224 * h + 64 * g + 64], lanes)
        )

    arrived(p1r, 0)
    acts = []
    for k in range(2):
        acc = gu[k, pl.ds(8 * s, 8)].astype(F32)
        for d in range(7):
            acc = acc + p1r[d, k].astype(F32)
        acts.append(acc * rt[pl.ds(8 * s, 8)])
    hb[...] = (jax.nn.gelu(acts[0], approximate=True) * acts[1]).astype(BF16)

    slot = jnp.where(c == half, 0, 1)
    place = hh.at[slot, pl.ds(8 * lax.rem(s, 4), 8)]

    @pl.when(c == half)
    def _():
        pltpu.make_async_copy(hb, place, rsem.at[2]).start()

    @pl.when(c != half)
    def _():
        send(hb, place, 2, src_peer(0, half))

    loop(SRC, lambda d: send(hb, place, 2, src_peer(d, half)))
    shares[1].wait()
    arrived(hh, 2)
    acc = jnp.zeros((HALF, 384), F32)
    for k in range(2):
        last = rows(hh[k, 28:32])
        keep = jnp.zeros_like(last)
        split = jnp.concatenate(
            [jnp.where((lanes >= 32 * g) & (lanes < 32 * g + 32), last, keep) for g in range(4)], axis=0
        )[0:HALF]
        lhs = jnp.concatenate([rows(hh[k, 0:14]), rows(hh[k, 14:28]), split], axis=1)
        acc = acc + dot(lhs, dwf[k])
    for j in range(2):
        ot[14 * j : 14 * j + 14] = tiles(acc[:, 128 * j : 128 * j + 128].astype(BF16))
    tail[0:224] = acc[:, 256:384]
    tail[224:256] = jnp.zeros((32, 128), F32)
    ot[28:32] = tiles(fold(lambda g: tail[64 * g : 64 * g + 64], lanes).astype(BF16))

    loop(32, lambda d: send(ot.at[lax.rem(q + d, 32)], p3r.at[d - 1], 3, q_peer(d)))
    arrived(p3r, 3)
    acc = ot[q].astype(F32)
    for d in range(31):
        acc = acc + p3r[d].astype(F32)
    gs[xy * 16 + z] = (rest[q] + acc).astype(BF16)

    mine = gs.at[xy * 16 + z]
    loop(ZN, lambda d: send(mine, mine, 4, z_peer(d)))
    arrived(gs.at[0:15], 4)
    block = gs.at[pl.ds(xy * 16, 16)]
    loop(16, lambda d: send(block, block, 5, xy_peer(d)))
    arrived(gs.at[0:240], 5)

    acc = jnp.zeros((HALF, 128), F32)
    rem = jnp.zeros((64, 128), F32)
    for k in range(SRC):
        for j in range(2):
            v = rows(gs[32 * k + 14 * j : 32 * k + 14 * j + 14]).astype(F32)
            acc = acc + v * v
        v = rows(gs[32 * k + 28 : 32 * k + 32]).astype(F32)
        rem = rem + v * v
    acc = acc + jnp.concatenate(
        [jnp.where((lanes >= 32 * g) & (lanes < 32 * g + 32), rem, 0.0) for g in range(4)], axis=0
    )[0:HALF]
    inv = lax.rsqrt(jnp.sum(acc, axis=1, keepdims=True) / D + eps_rms)
    tall = lane_group((HALF, 128))

    def turn(v, by):
        by = by % 128
        return v if by == 0 else pltpu.roll(v, by, 1)

    for k in range(SRC):
        m, base = k % 4, 9 * (k // 4)
        a0 = turn(rows(gs[32 * k : 32 * k + 14]).astype(F32) * inv, 32 * m)
        a1 = turn(rows(gs[32 * k + 14 : 32 * k + 28]).astype(F32) * inv, 32 * m)
        last = rows(gs[32 * k + 28 : 32 * k + 32]).astype(F32)
        rem = jnp.concatenate([turn(last, 32 * m - 32 * g) for g in range(4)], axis=0)[0:HALF] * inv
        if m == 0:
            first, second = a0, a1
        else:
            first = jnp.where(tall < 32 * m, carry, a0)
            second = jnp.where(tall < 32 * m, a0, a1)
        carry = jnp.where(tall < 32 * m, a1, rem)
        for at, v in ((2 * m, first), (2 * m + 1, second)) + (((8, carry),) if m == 3 else ()):
            ss[14 * (base + at) : 14 * (base + at) + 14] = tiles(v.astype(BF16))

    def cols_of(ref, p):
        return jnp.concatenate([rows(ref[28 * p : 28 * p + 14]), rows(ref[28 * p + 14 : 28 * p + 28])], axis=1)

    for k in (0, 2, 3):
        shares[k].wait()
    acc = jnp.zeros((HALF, 256), F32)
    for p in range(9):
        rhs = jnp.concatenate([ew[0, 256 * p : 256 * p + 256], ew[1, 256 * p : 256 * p + 256]], axis=1)
        acc = acc + dot(cols_of(ss, p), rhs)
    acc = acc + jnp.concatenate([ebx[0, 0:1], ebx[1, 0:1]], axis=1)
    pa[...] = acc
    latents = jnp.maximum(acc, 0.0)
    lat = latents.astype(BF16)
    for p in range(9):
        rhs = jnp.concatenate([dcw[0, :, 256 * p : 256 * p + 256], dcw[1, :, 256 * p : 256 * p + 256]], axis=0)
        r = dot(lat, rhs).astype(BF16)
        tt[28 * p : 28 * p + 14] = tiles(r[:, 0:128])
        tt[28 * p + 14 : 28 * p + 28] = tiles(r[:, 128:256])

    loop(16, lambda d: send(tt.at[pl.ds(16 * lax.rem(xy + d, 16), 16)], p5r.at[d - 1], 6, xy_peer(d)))
    lat_t[...] = jnp.concatenate([latents, jnp.zeros((32, 256), F32)], axis=0).T.astype(BF16)
    for p in range(18):
        v = rows(ss[14 * p : 14 * p + 14]).astype(F32)
        st[128 * p : 128 * p + 128] = jnp.concatenate([v, jnp.zeros((32, 128), F32)], axis=0).T.astype(BF16)
    arrived(p5r, 6)

    def add_up(k, carry):
        acc = tt[16 * xy + k].astype(F32)
        for d in range(15):
            acc = acc + p5r[d, k].astype(F32)
        aa[k] = acc.astype(BF16)
        return carry

    lax.fori_loop(0, 16, add_up, 0)
    loop(ZN, lambda d: send(aa.at[lax.rem(z + d, ZN)], p5z.at[d - 1], 7, z_peer(d)))
    arrived(p5z, 7)
    acc = aa[z].astype(F32)
    for d in range(15):
        acc = acc + p5z[d].astype(F32)
    t = xy * 16 + z
    col = jnp.minimum(lax.div(t, 14), 17)
    row = lax.rem(t, 14)
    err = (acc + bias[col, 0:1] - ss[t].astype(F32)).astype(BF16)
    tw = twb[pl.ds(pl.multiple_of(off + 16 * row, 16), 16)]
    ee[t] = (2.0 * tw * err.astype(F32)).astype(BF16)
    mine2 = ee.at[t]
    loop(ZN, lambda d: send(mine2, mine2, 8, z_peer(d)))
    arrived(ee.at[0:15], 8)
    block2 = ee.at[pl.ds(xy * 16, 16)]
    loop(16, lambda d: send(block2, block2, 9, xy_peer(d)))
    arrived(ee.at[0:240], 9)

    lt = lat_t[:, 0:HALF]
    acc = jnp.zeros((HALF, 256), F32)
    for p in range(9):
        r = dot(lt, cols_of(ee, p))
        dg[:, 256 * p : 256 * p + 256] = r[0:128]
        dgs[:, 256 * p : 256 * p + 256] = r[128:256].astype(BF16)
    send(dgs, dgr, 10, other)
    for p in range(9):
        rhs = jnp.concatenate([dcw[0, :, 256 * p : 256 * p + 256], dcw[1, :, 256 * p : 256 * p + 256]], axis=0)
        acc = acc + dot(cols_of(ee, p), rhs, 1, 1)
    tw = l1_coeff * twb[pl.ds(off, HALF)]
    acc = acc + jnp.concatenate([tw, tw], axis=1)
    pg = jnp.where(pa[...] > 0.0, acc, 0.0).astype(BF16)
    for p in range(9):
        r = dot(st[256 * p : 256 * p + 256, 0:HALF], pg)
        eg[256 * p : 256 * p + 256] = r[:, 0:128]
        egs[256 * p : 256 * p + 256] = r[:, 128:256].astype(BF16)
    send(egs, egr, 11, other)
    arrived(dgr, 10)
    acc = jnp.zeros((8, 128), F32)
    for p in range(18):
        v = dg[:, 128 * p : 128 * p + 128] + dgr[:, 128 * p : 128 * p + 128].astype(F32)
        dg[:, 128 * p : 128 * p + 128] = v
        acc = acc + jnp.sum((v * v).reshape(16, 8, 128), axis=0)
    arrived(egr, 11)
    for p in range(18):
        v = eg[128 * p : 128 * p + 128] + egr[128 * p : 128 * p + 128].astype(F32)
        eg[128 * p : 128 * p + 128] = v
        acc = acc + jnp.sum((v * v).reshape(16, 8, 128), axis=0)

    n7[0] = acc
    loop(ZN, lambda d: send(n7.at[0], n7z.at[d - 1], 12, z_peer(d)))
    for k in range(3, 7):
        loads[k].wait()
    arrived(n7z, 12)
    for d in range(15):
        acc = acc + n7z[d]
    n7[1] = acc
    loop(16, lambda d: send(n7.at[1], n7x.at[d - 1], 13, xy_peer(d)))
    arrived(n7x, 13)
    for d in range(15):
        acc = acc + n7x[d]
    n7[2] = acc
    send(n7.at[2], n7c, 14, other)
    arrived(n7c, 14)
    acc = acc + n7c[...]
    clip = lax.rsqrt(jnp.sum(acc, keepdims=True) + 1e-12)

    for p in range(18):
        at = slice(128 * p, 128 * p + 128)
        do[:, at] = adam(dg[:, at], df[:, at], ds[:, at], clip)
        eo[at] = adam(eg[at], ef[at], es[at], clip)

    left(p1r, 0)
    left(sqr, 1)

    @pl.when(c == half)
    def _():
        left(hh.at[0, 0:28], 2)
        left(hh.at[1, 0:28], 2)

    @pl.when(c != half)
    def _():
        left(hh, 2)

    left(p3r, 3)
    left(gs.at[0:15], 4)
    left(gs.at[0:240], 5)
    left(p5r, 6)
    left(p5z, 7)
    left(ee.at[0:15], 8)
    left(ee.at[0:240], 9)
    left(dgs, 10)
    left(egs, 11)
    left(n7z, 12)
    left(n7x, 13)
    left(n7c, 14)


def local(
    residual, token_ids, ffn_gain, gate_w, up_w, down_w, enc_w, enc_bias, dec_w, dec_bias,
    enc_first, enc_second, dec_first, dec_second,
):
    vm = pl.BlockSpec(memory_space=pltpu.VMEM)
    hbm = pl.BlockSpec(memory_space=pl.ANY)
    V = pltpu.VMEM
    scratch = [
        V((W, W), BF16), V((2, D, 128), BF16), V((2, 128, D), BF16),
        V((D, 128), BF16), V((D, 128), BF16), V((128, D), BF16), V((128, D), BF16), V((2, 8, 128), F32),
        V((512, 128), F32), V((64, 16, 128), F32), V((2, 64, 16, 128), BF16), V((7, 2, 8, 16, 128), BF16),
        V((8, 128), F32), V((7, 8, 128), F32), V((8, 16, 128), BF16), V((2, 32, 16, 128), BF16),
        V((2, 384, 384), BF16), V((512, 128), F32), V((32, 16, 128), F32), V((32, 16, 128), BF16),
        V((31, 16, 128), BF16),
        V((256, 16, 128), BF16), V((256, 16, 128), BF16), V((512, 128), F32), V((18, 8, 128), F32),
        V((HALF, 256), F32), V((256, 256), BF16), V((256, 16, 128), BF16), V((15, 16, 16, 128), BF16),
        V((16, 16, 128), BF16), V((15, 16, 128), BF16), V((256, 16, 128), BF16), V((D, 256), BF16),
        V((128, D), F32), V((128, D), BF16), V((128, D), BF16),
        V((D, 128), F32), V((D, 128), BF16), V((D, 128), BF16),
        V((3, 8, 128), F32), V((15, 8, 128), F32), V((15, 8, 128), F32), V((8, 128), F32),
        pltpu.SemaphoreType.DMA((7,)), pltpu.SemaphoreType.DMA((4,)), pltpu.SemaphoreType.DMA((4,)),
        pltpu.SemaphoreType.DMA((15,)), pltpu.SemaphoreType.DMA((15,)),
    ]
    return pl.pallas_call(
        kernel,
        out_shape=(jax.ShapeDtypeStruct((D, 128), BF16), jax.ShapeDtypeStruct((128, D), BF16)),
        in_specs=[vm, vm, vm, vm, vm, hbm, hbm, vm, hbm, vm, hbm, hbm, hbm, hbm],
        out_specs=(vm, vm),
        scratch_shapes=scratch,
        compiler_params=pltpu.CompilerParams(
            collective_id=0, has_side_effects=True, vmem_limit_bytes=48 << 20
        ),
    )(
        residual, token_ids.reshape(1, TOK), ffn_gain.reshape(1, W), gate_w, up_w, down_w, enc_w,
        enc_bias.reshape(1, 128), dec_w, dec_bias.reshape(1, D), enc_first, enc_second, dec_first, dec_second,
    )


def solution(mesh):
    in_specs = (
        P(None, "src"),
        P(),
        P("src"),
        P("src", "feat"),
        P("src", "feat"),
        P("feat", "src"),
        P(None, ("src", "feat")),
        P(("src", "feat")),
        P(("src", "feat"), None),
        P(),
        P(None, ("src", "feat")),
        P(None, ("src", "feat")),
        P(("src", "feat"), None),
        P(("src", "feat"), None),
    )
    out_specs = (P(None, ("src", "feat")), P(("src", "feat"), None))
    return jax.shard_map(local, mesh=mesh, in_specs=in_specs, out_specs=out_specs, check_vma=False)
```

```python
import functools

import jax
import jax.numpy as jnp
from jax import lax
from jax.experimental import pallas as pl
from jax.experimental.pallas import tpu as pltpu
from jax.sharding import PartitionSpec as P

SPECIAL = 4
TOK = 448
HALF = 224
D = 2304
W = 288
ZN = 16
SRC = 8
FEAT = 64

eps_rms = 1e-06
beta_one = 0.9
beta_two = 0.999
adam_count = 100.0
l1_coeff = 0.2

F32 = jnp.float32
BF16 = jnp.bfloat16


def tiles(v):
    return v.reshape(v.shape[0] // 16, 16, 128)


def rows(v):
    return v.reshape(v.shape[0] * 16, 128)


def dot(a, b, ca=1, cb=0):
    return lax.dot_general(a, b, (((ca,), (cb,)), ((), ())), preferred_element_type=F32)


def lane_group(shape):
    return lax.broadcasted_iota(jnp.int32, shape, len(shape) - 1)


def fold(read, lanes):
    out = read(3)
    for g in (2, 1, 0):
        out = jnp.where(lanes < 32 * (g + 1), read(g), out)
    return out


FAR = (8, 9, 7, 10, 6, 11, 5, 12, 4, 13, 3)
GROUPS = ((3, 5), (12, 14), (5, 7), (10, 12), (7, 10))
GROUP_OF = {place: g for g, (lo, hi) in enumerate(GROUPS) for place in range(lo, hi)}


def adam(grad, first, second, clip):
    corr_one = 1.0 - beta_one**adam_count
    corr_two = 1.0 - beta_two**adam_count
    scaled_grad = clip * grad
    mean = (beta_one / corr_one) * first.astype(F32) + ((1.0 - beta_one) / corr_one) * scaled_grad
    power = (beta_two / corr_two) * second.astype(F32) + ((1.0 - beta_two) / corr_two) * (scaled_grad * scaled_grad)
    return (mean / (jnp.sqrt(power) + 1e-08)).astype(BF16)


def adam_kernel(clip, eg, ef, es, dg, df, ds, eo_h, do_h, eo, do, sem):
    scale = clip[0:1, 0:1]
    copies = []
    for p in range(6):
        at = slice(384 * p, 384 * p + 384)
        do[:, at] = adam(dg[:, at], df[:, at], ds[:, at], scale)
        copies.append(pltpu.make_async_copy(do.at[:, at], do_h.at[:, at], sem.at[2 * p]))
        copies[-1].start()
        eo[at] = adam(eg[at], ef[at], es[at], scale)
        copies.append(pltpu.make_async_copy(eo.at[at], eo_h.at[at], sem.at[2 * p + 1]))
        copies[-1].start()
    for cp in copies:
        cp.wait()


def kernel(
    res_t, tok, gain, gw, uw, dw_h, ew_h, eb, dcw_h, db, ef_h, es_h, df_h, ds_h,
    eg, dg, clip, ef, es, df, ds,
    dw, ew, dcw, ebx,
    rf, rn, rt, gu, p1r, sqs, sqr, hb, hh, dwf, tail, rest, ot, p3r,
    gs, ss, twb, bias, pa, lat_t, tt, p5r, zb, own, aa, p5z, ee, st,
    dgs, dgr, egs, egr, n7, n7z, n7x,
    lsem, wsend, wrecv, ssem, rsem,
):
    s = lax.axis_index("src")
    f = lax.axis_index("feat")
    c = lax.rem(f, 2)
    q = lax.div(f, 2)
    z = lax.rem(q, ZN)
    yhi = lax.div(q, ZN)
    xy = s * 2 + yhi
    half = lax.div(s, 4)

    def to(src, feat):
        return {"device_id": (src, feat), "device_id_type": pl.DeviceIdType.MESH}

    other = to(s, q * 2 + 1 - c)

    def src_peer(d, core):
        return to(lax.rem(s + d, SRC), q * 2 + core)

    def q_peer(d):
        return to(s, lax.rem(q + d, 32) * 2 + c)

    def z_peer(d):
        return to(s, (yhi * ZN + lax.rem(z + d, ZN)) * 2 + c)

    def xy_peer(d, core=c):
        i = lax.rem(xy + d, 16)
        return to(lax.div(i, 2), (lax.rem(i, 2) * ZN + z) * 2 + core)

    def loop(n, fn):
        def body(d, carry):
            fn(d)
            return carry

        lax.fori_loop(1, n, body, 0)

    def send(src, dst, k, where, at=None):
        pltpu.make_async_remote_copy(
            src_ref=src, dst_ref=dst, send_sem=ssem.at[k], recv_sem=rsem.at[k if at is None else at], **where
        ).start()

    def arrived(ref, k):
        pltpu.make_async_copy(ref, ref, rsem.at[k]).wait()

    def left(ref, k):
        pltpu.make_async_copy(ref, ref, ssem.at[k]).wait()

    place_of = [lax.rem(k + ZN - z, ZN) for k in range(ZN)]

    def far_first(n, d):
        step = lax.div(d, 2)
        return n // 2 + jnp.where(lax.rem(d, 2) == 0, step, -step)

    def gather(buf, k, m):
        mine = buf.at[xy, 0]
        for d in FAR:
            send(mine, buf.at[xy, ZN - d], k, z_peer(d), m + GROUP_OF[ZN - d])
        loop(16, lambda d: send(mine, mine, k + 1, xy_peer(d), m + 5))

        def onward(g):
            lo, hi = GROUPS[g]
            arrived(buf.at[0, lo:hi], m + g)
            part = buf.at[xy, lo:hi]
            loop(16, lambda d: send(part, part, k + 1, xy_peer(d), m + 6))

        onward(0)
        onward(1)
        arrived(buf.at[0, 0:15], m + 5)
        for d in (2, 14, 1, 15):
            send(buf.at[:, 0], buf.at[:, ZN - d], k + 2, z_peer(d), m + 7)
        onward(2)
        onward(3)
        onward(4)
        arrived(buf.at[0:15, 0:11], m + 6)
        arrived(buf.at[:, 0:4], m + 7)

    def gathered(buf, k):
        left(buf.at[0, 0:11], k)
        left(buf.at[0:15, 0:12], k + 1)
        left(buf.at[:, 0:4], k + 2)

    barrier = pltpu.get_barrier_semaphore()
    pl.semaphore_signal(barrier, inc=1, **other)

    def greet(d):
        pl.semaphore_signal(barrier, inc=1, **src_peer(d, c))
        pl.semaphore_signal(barrier, inc=1, **src_peer(d, 1 - c))
        for core in (c, 1 - c):
            pl.semaphore_signal(
                barrier, inc=1, **to(lax.rem(s + d, SRC), (lax.rem(yhi + 1, 2) * ZN + z) * 2 + core)
            )

    pl.semaphore_signal(barrier, inc=1, **to(s, (lax.rem(yhi + 1, 2) * ZN + z) * 2 + 1 - c))
    loop(SRC, greet)
    loop(32, lambda d: pl.semaphore_signal(barrier, inc=1, **q_peer(d)))

    loads = []
    for k, (src, dst) in enumerate(
        ((dw_h, dw), (ew_h, ew.at[0]), (dcw_h, dcw.at[0]), (ef_h, ef), (es_h, es), (df_h, df), (ds_h, ds))
    ):
        cp = pltpu.make_async_copy(src, dst, lsem.at[k])
        cp.start()
        loads.append(cp)

    lanes = lane_group((64, 128))
    pick = jnp.where(
        jnp.bitwise_and(lane_group((32, 128)), 31) == lax.broadcasted_iota(jnp.int32, (32, 128), 0), 1.0, 0.0
    ).astype(BF16)

    turned = jnp.concatenate([res_t[...].astype(F32), jnp.zeros((W, 64), F32)], axis=1)
    rf[...] = turned.T
    xg = (rf[0:448] * gain[...].astype(F32).reshape(1, W)).astype(BF16)
    for k, w in enumerate((gw, uw)):
        main = dot(xg, w[:, 0:256])
        spread = dot(w[:, 256:288], pick).astype(BF16)
        tail[0:448] = dot(xg, spread)
        tail[448:512] = jnp.zeros((64, 128), F32)
        for h in range(2):
            for j in range(2):
                gu[k, h * 32 + 14 * j : h * 32 + 14 * j + 14] = tiles(
                    main[224 * h : 224 * h + 224, 128 * j : 128 * j + 128].astype(BF16)
                )
            part = fold(lambda g: tail[224 * h + 64 * g : 224 * h + 64 * g + 64], lanes)
            gu[k, h * 32 + 28 : h * 32 + 32] = tiles(part.astype(BF16))
    squares = jnp.sum(turned * turned, axis=0, keepdims=True)
    sqs[...] = jnp.concatenate(
        [squares[:, 128 * k : 128 * k + 128] for k in range(4)] + [jnp.zeros((4, 128), F32)], axis=0
    )

    pl.semaphore_wait(barrier, 61)

    def send_p1(d):
        t = lax.rem(s + d, SRC)
        send(gu.at[:, pl.ds(8 * t, 8)], p1r.at[d - 1], 0, src_peer(d, c))
        send(sqs, sqr.at[d - 1], 1, src_peer(d, c))

    loop(SRC, send_p1)

    ids = tok[...]
    live = jnp.where(ids >= SPECIAL, 1.0, 0.0)
    weight = live / jnp.maximum(jnp.sum(live), 1.0)
    weight = jnp.concatenate([weight, jnp.zeros((1, 64), F32)], axis=1)
    weight = jnp.concatenate(
        [weight[:, 128 * k : 128 * k + 128] for k in range(4)] + [jnp.zeros((124, 128), F32)], axis=0
    ).T
    for k in range(4):
        twb[128 * k : 128 * k + 128] = jnp.broadcast_to(weight[:, k : k + 1], (128, 128))
    for k in range(18):
        bias[k] = jnp.broadcast_to(db[128 * k : 128 * k + 128].astype(F32).reshape(1, 128), (8, 128))
    ebx[0] = jnp.broadcast_to(eb[...].astype(F32), (8, 128))

    def share(ref, k):
        return pltpu.make_async_remote_copy(
            src_ref=ref.at[0], dst_ref=ref.at[1], send_sem=wsend.at[k], recv_sem=wrecv.at[k], **other
        )

    shares = [share(ebx, 0), share(dwf, 1), share(ew, 2), share(dcw, 3)]
    shares[0].start()
    loads[0].wait()
    spread = dot(dw[:, 256:288], pick).astype(BF16)
    dwf[0, 0:256, 0:256] = dw[0:256, 0:256]
    dwf[0, 0:256, 256:384] = spread[0:256]
    for g in range(4):
        dwf[0, 256 + 32 * g : 288 + 32 * g, 0:256] = dw[256:288, 0:256]
        dwf[0, 256 + 32 * g : 288 + 32 * g, 256:384] = spread[256:288]
    shares[1].start()
    loads[1].wait()
    shares[2].start()
    loads[2].wait()
    shares[3].start()

    off = pl.multiple_of(HALF * c, 32)
    for j in range(2):
        rest[14 * j : 14 * j + 14] = tiles(rf[pl.ds(off, HALF), 128 * j : 128 * j + 128])
    tail[0:448] = dot(rf[0:448, 256:288].astype(BF16), pick)
    tail[448:512] = jnp.zeros((64, 128), F32)
    rest[28:32] = tiles(fold(lambda g: tail[pl.ds(off + 64 * g, 64)], lanes))
    ss[252:256] = jnp.zeros((4, 16, 128), BF16)
    for k in range(12, 16):
        tt[15, place_of[k]] = jnp.zeros((16, 128), BF16)

    arrived(sqr, 1)
    total = sqs[...]
    for d in range(7):
        total = total + sqr[d]
    inv = lax.rsqrt(total / D + eps_rms)
    inv = jnp.concatenate([inv, jnp.zeros((120, 128), F32)], axis=0).T
    for k in range(4):
        rn[128 * k : 128 * k + 128] = jnp.broadcast_to(inv[:, k : k + 1], (128, 128))
    for h in range(2):
        for j in range(2):
            rt[h * 32 + 14 * j : h * 32 + 14 * j + 14] = tiles(rn[224 * h : 224 * h + 224])
        rt[h * 32 + 28 : h * 32 + 32] = tiles(
            fold(lambda g: rn[224 * h + 64 * g : 224 * h + 64 * g + 64], lanes)
        )

    arrived(p1r, 0)
    acts = []
    for k in range(2):
        acc = gu[k, pl.ds(8 * s, 8)].astype(F32)
        for d in range(7):
            acc = acc + p1r[d, k].astype(F32)
        acts.append(acc * rt[pl.ds(8 * s, 8)])
    hb[...] = (jax.nn.gelu(acts[0], approximate=True) * acts[1]).astype(BF16)

    slot = jnp.where(c == half, 0, 1)
    place = hh.at[slot, pl.ds(8 * lax.rem(s, 4), 8)]

    @pl.when(c == half)
    def _():
        pltpu.make_async_copy(hb, place, rsem.at[2]).start()

    @pl.when(c != half)
    def _():
        send(hb, place, 2, src_peer(0, half))

    loop(SRC, lambda d: send(hb, place, 2, src_peer(d, half)))
    shares[1].wait()
    arrived(hh, 2)
    acc = jnp.zeros((HALF, 384), F32)
    for k in range(2):
        last = rows(hh[k, 28:32])
        keep = jnp.zeros_like(last)
        split = jnp.concatenate(
            [jnp.where((lanes >= 32 * g) & (lanes < 32 * g + 32), last, keep) for g in range(4)], axis=0
        )[0:HALF]
        lhs = jnp.concatenate([rows(hh[k, 0:14]), rows(hh[k, 14:28]), split], axis=1)
        acc = acc + dot(lhs, dwf[k])
    for j in range(2):
        ot[14 * j : 14 * j + 14] = tiles(acc[:, 128 * j : 128 * j + 128].astype(BF16))
    tail[0:224] = acc[:, 256:384]
    tail[224:256] = jnp.zeros((32, 128), F32)
    ot[28:32] = tiles(fold(lambda g: tail[64 * g : 64 * g + 64], lanes).astype(BF16))


    def send_p3(d):
        k = far_first(32, d)
        send(ot.at[lax.rem(q + k, 32)], p3r.at[k - 1], 3, q_peer(k))

    loop(32, send_p3)
    arrived(p3r, 3)
    acc = ot[q].astype(F32)
    for d in range(31):
        acc = acc + p3r[d].astype(F32)
    gs[xy, 0] = (rest[q] + acc).astype(BF16)

    gather(gs, 4, 14)

    def picked(buf, first, n):
        return jnp.concatenate([buf[t // 16, place_of[t % 16]] for t in range(first, first + n)], axis=0)

    acc = jnp.zeros((HALF, 128), F32)
    rem = jnp.zeros((64, 128), F32)
    for k in range(SRC):
        for j in range(2):
            v = picked(gs, 32 * k + 14 * j, 14).astype(F32)
            acc = acc + v * v
        v = picked(gs, 32 * k + 28, 4).astype(F32)
        rem = rem + v * v
    acc = acc + jnp.concatenate(
        [jnp.where((lanes >= 32 * g) & (lanes < 32 * g + 32), rem, 0.0) for g in range(4)], axis=0
    )[0:HALF]
    inv = lax.rsqrt(jnp.sum(acc, axis=1, keepdims=True) / D + eps_rms)
    tall = lane_group((HALF, 128))

    def turn(v, by):
        by = by % 128
        return v if by == 0 else pltpu.roll(v, by, 1)

    for k in range(SRC):
        m, base = k % 4, 9 * (k // 4)
        a0 = turn(picked(gs, 32 * k, 14).astype(F32) * inv, 32 * m)
        a1 = turn(picked(gs, 32 * k + 14, 14).astype(F32) * inv, 32 * m)
        last = picked(gs, 32 * k + 28, 4).astype(F32)
        rem = jnp.concatenate([turn(last, 32 * m - 32 * g) for g in range(4)], axis=0)[0:HALF] * inv
        if m == 0:
            first, second = a0, a1
        else:
            first = jnp.where(tall < 32 * m, carry, a0)
            second = jnp.where(tall < 32 * m, a0, a1)
        carry = jnp.where(tall < 32 * m, a1, rem)
        for at, v in ((2 * m, first), (2 * m + 1, second)) + (((8, carry),) if m == 3 else ()):
            ss[14 * (base + at) : 14 * (base + at) + 14] = tiles(v.astype(BF16))

    def cols_of(ref, p):
        return jnp.concatenate([rows(ref[28 * p : 28 * p + 14]), rows(ref[28 * p + 14 : 28 * p + 28])], axis=1)

    for k in (0, 2, 3):
        shares[k].wait()
    acc = jnp.zeros((HALF, 256), F32)
    for p in range(9):
        rhs = jnp.concatenate([ew[0, 256 * p : 256 * p + 256], ew[1, 256 * p : 256 * p + 256]], axis=1)
        acc = acc + dot(cols_of(ss, p), rhs)
    acc = acc + jnp.concatenate([ebx[0, 0:1], ebx[1, 0:1]], axis=1)
    pa[...] = acc
    latents = jnp.maximum(acc, 0.0)
    lat = latents.astype(BF16)
    for p in range(9):
        rhs = jnp.concatenate([dcw[0, :, 256 * p : 256 * p + 256], dcw[1, :, 256 * p : 256 * p + 256]], axis=0)
        r = dot(lat, rhs).astype(BF16)
        for t in range(28 * p, 28 * p + 28):
            k = t - 28 * p
            tt[t // 16, place_of[t % 16]] = r[16 * (k % 14) : 16 * (k % 14) + 16, 128 * (k // 14) : 128 * (k // 14) + 128]

    def across(g):
        lo, hi = GROUPS[g]
        loop(
            16,
            lambda d: send(
                tt.at[lax.rem(xy + d, 16), lo:hi], p5r.at[d - 1, lo:hi], 7, xy_peer(d), 22 + g
            ),
        )

    across(4)
    for k, d in enumerate((2, 14, 1, 15)):
        send(tt.at[:, d], zb.at[k], 8, z_peer(d), 28)
    for g in (2, 3, 0, 1):
        across(g)
    lat_t[...] = jnp.concatenate([latents, jnp.zeros((32, 256), F32)], axis=0).T.astype(BF16)
    for p in range(18):
        v = rows(ss[14 * p : 14 * p + 14]).astype(F32)
        st[128 * p : 128 * p + 128] = jnp.concatenate([v, jnp.zeros((32, 128), F32)], axis=0).T.astype(BF16)

    def onward(g):
        lo, hi = GROUPS[g]
        arrived(p5r.at[:, lo:hi], 22 + g)
        for k in range(lo, hi):
            acc = tt[xy, k].astype(F32)
            for d in range(15):
                acc = acc + p5r[d, k].astype(F32)
            aa[k] = acc.astype(BF16)
            send(aa.at[k], p5z.at[k - 3], 9, z_peer(k), 29)

    onward(4)
    arrived(zb, 28)
    for k in range(16):
        acc = tt[k, 0].astype(F32)
        for d in range(4):
            acc = acc + zb[d, k].astype(F32)
        own[k] = acc.astype(BF16)
    loop(16, lambda d: send(own.at[lax.rem(xy + d, 16)], p5r.at[d - 1, 0], 7, xy_peer(d), 27))
    for g in (2, 3, 0, 1):
        onward(g)
    arrived(p5r.at[:, 0], 27)
    acc = own[xy].astype(F32)
    for d in range(15):
        acc = acc + p5r[d, 0].astype(F32)
    arrived(p5z, 29)
    for d in range(11):
        acc = acc + p5z[d].astype(F32)
    t = xy * 16 + z
    col = jnp.minimum(lax.div(t, 14), 17)
    row = lax.rem(t, 14)
    err = (acc + bias[col, 0:1] - ss[t].astype(F32)).astype(BF16)
    tw = twb[pl.ds(pl.multiple_of(off + 16 * row, 16), 16)]
    ee[xy, 0] = (2.0 * tw * err.astype(F32)).astype(BF16)
    gather(ee, 10, 30)

    def err_cols(p):
        return jnp.concatenate([picked(ee, 28 * p, 14), picked(ee, 28 * p + 14, 14)], axis=1)

    acc = jnp.zeros((HALF, 256), F32)
    for p in range(9):
        rhs = jnp.concatenate([dcw[0, :, 256 * p : 256 * p + 256], dcw[1, :, 256 * p : 256 * p + 256]], axis=0)
        acc = acc + dot(err_cols(p), rhs, 1, 1)
    tw = l1_coeff * twb[pl.ds(off, HALF)]
    acc = acc + jnp.concatenate([tw, tw], axis=1)
    pg = jnp.where(pa[...] > 0.0, acc, 0.0).astype(BF16)
    for p in range(9):
        r = dot(st[256 * p : 256 * p + 256, 0:HALF], pg)
        eg[256 * p : 256 * p + 256] = r[:, 0:128]
        egs[256 * p : 256 * p + 256] = r[:, 128:256].astype(BF16)
        if p % 3 == 2:
            part = pl.ds(768 * (p // 3), 768)
            send(egs.at[part], egr.at[part], 13, other, 38 + p // 3)
    lt = lat_t[:, 0:HALF]
    for p in range(9):
        r = dot(lt, err_cols(p))
        dg[:, 256 * p : 256 * p + 256] = r[0:128]
        dgs[:, 256 * p : 256 * p + 256] = r[128:256].astype(BF16)
        if p % 3 == 2:
            part = pl.ds(768 * (p // 3), 768)
            send(dgs.at[:, part], dgr.at[:, part], 14, other, 41 + p // 3)
    acc = jnp.zeros((8, 128), F32)
    for p in range(18):
        if p % 6 == 0:
            arrived(egr.at[0:768], 38 + p // 6)
        v = eg[128 * p : 128 * p + 128] + egr[128 * p : 128 * p + 128].astype(F32)
        eg[128 * p : 128 * p + 128] = v
        acc = acc + jnp.sum((v * v).reshape(16, 8, 128), axis=0)
    for p in range(18):
        if p % 6 == 0:
            arrived(dgr.at[:, 0:768], 41 + p // 6)
        v = dg[:, 128 * p : 128 * p + 128] + dgr[:, 128 * p : 128 * p + 128].astype(F32)
        dg[:, 128 * p : 128 * p + 128] = v
        acc = acc + jnp.sum((v * v).reshape(16, 8, 128), axis=0)

    n7[0] = acc

    def send_n(d):
        k = far_first(ZN, d)
        send(n7.at[0], n7z.at[k - 1], 15, z_peer(k), 44)

    loop(ZN, send_n)
    arrived(n7z, 44)
    for d in range(15):
        acc = acc + n7z[d]
    n7[1] = acc

    def send_xy(d):
        send(n7.at[1], n7x.at[d - 1], 16, xy_peer(d), 45)
        send(n7.at[1], n7x.at[d + 15], 16, xy_peer(d, 1 - c), 45)

    loop(16, send_xy)
    send(n7.at[1], n7x.at[15], 16, other, 45)
    arrived(n7x, 45)
    for d in range(31):
        acc = acc + n7x[d]
    clip[...] = jnp.broadcast_to(lax.rsqrt(jnp.sum(acc, keepdims=True) + 1e-12), (8, 128))
    for k in range(3, 7):
        loads[k].wait()

    left(p1r, 0)
    left(sqr, 1)

    @pl.when(c == half)
    def _():
        left(hh.at[0, 0:28], 2)
        left(hh.at[1, 0:28], 2)

    @pl.when(c != half)
    def _():
        left(hh, 2)

    left(p3r, 3)
    gathered(gs, 4)
    left(p5r.at[:, 0:12], 7)
    left(zb, 8)
    left(p5z, 9)
    gathered(ee, 10)
    left(egs, 13)
    left(dgs, 14)
    left(n7z, 15)
    left(n7x, 16)


def local(
    residual, token_ids, ffn_gain, gate_w, up_w, down_w, enc_w, enc_bias, dec_w, dec_bias,
    enc_first, enc_second, dec_first, dec_second,
):
    vm = pl.BlockSpec(memory_space=pltpu.VMEM)
    hbm = pl.BlockSpec(memory_space=pl.ANY)
    V = pltpu.VMEM
    scratch = [
        V((W, W), BF16), V((2, D, 128), BF16), V((2, 128, D), BF16), V((2, 8, 128), F32),
        V((512, W), F32), V((512, 128), F32), V((64, 16, 128), F32), V((2, 64, 16, 128), BF16),
        V((7, 2, 8, 16, 128), BF16), V((8, 128), F32), V((7, 8, 128), F32), V((8, 16, 128), BF16),
        V((2, 32, 16, 128), BF16), V((2, 384, 384), BF16), V((512, 128), F32), V((32, 16, 128), F32),
        V((32, 16, 128), BF16), V((31, 16, 128), BF16),
        V((16, 16, 16, 128), BF16), V((256, 16, 128), BF16), V((512, 128), F32), V((18, 8, 128), F32),
        V((HALF, 256), F32), V((256, 256), BF16), V((16, 16, 16, 128), BF16), V((15, 16, 16, 128), BF16),
        V((4, 16, 16, 128), BF16), V((16, 16, 128), BF16), V((16, 16, 128), BF16), V((11, 16, 128), BF16),
        V((16, 16, 16, 128), BF16), V((D, 256), BF16),
        V((128, D), BF16), V((128, D), BF16), V((D, 128), BF16), V((D, 128), BF16),
        V((2, 8, 128), F32), V((15, 8, 128), F32), V((31, 8, 128), F32),
        pltpu.SemaphoreType.DMA((7,)), pltpu.SemaphoreType.DMA((4,)), pltpu.SemaphoreType.DMA((4,)),
        pltpu.SemaphoreType.DMA((17,)), pltpu.SemaphoreType.DMA((46,)),
    ]
    operands = [
        pltpu.with_memory_space_constraint(v, pltpu.HBM)
        for v in (
            residual.T, token_ids.reshape(1, TOK), ffn_gain, gate_w, up_w, down_w, enc_w,
            enc_bias.reshape(1, 128), dec_w, dec_bias, enc_first, enc_second, dec_first, dec_second,
        )
    ]
    tall, flat = jax.ShapeDtypeStruct((D, 128), BF16), jax.ShapeDtypeStruct((128, D), BF16)
    enc_grad, dec_grad, clip, enc_one, enc_two, dec_one, dec_two = pl.pallas_call(
        kernel,
        out_shape=(
            jax.ShapeDtypeStruct((D, 128), F32),
            jax.ShapeDtypeStruct((128, D), F32),
            jax.ShapeDtypeStruct((8, 128), F32),
            tall, tall, flat, flat,
        ),
        in_specs=[vm, vm, vm, vm, vm, hbm, hbm, vm, hbm, vm, hbm, hbm, hbm, hbm],
        out_specs=(vm,) * 7,
        scratch_shapes=scratch,
        compiler_params=pltpu.CompilerParams(
            collective_id=0, has_side_effects=True, vmem_limit_bytes=32 << 20
        ),
    )(*operands)
    return pl.pallas_call(
        adam_kernel,
        out_shape=(tall, flat),
        in_specs=[vm] * 7,
        out_specs=(hbm, hbm),
        scratch_shapes=[V((D, 128), BF16), V((128, D), BF16), pltpu.SemaphoreType.DMA((12,))],
        compiler_params=pltpu.CompilerParams(vmem_limit_bytes=16 << 20),
    )(clip, enc_grad, enc_one, enc_two, dec_grad, dec_one, dec_two)


def solution(mesh):
    in_specs = (
        P(None, "src"),
        P(),
        P("src"),
        P("src", "feat"),
        P("src", "feat"),
        P("feat", "src"),
        P(None, ("src", "feat")),
        P(("src", "feat")),
        P(("src", "feat"), None),
        P(),
        P(None, ("src", "feat")),
        P(None, ("src", "feat")),
        P(("src", "feat"), None),
        P(("src", "feat"), None),
    )
    out_specs = (P(None, ("src", "feat")), P(("src", "feat"), None))
    return jax.shard_map(local, mesh=mesh, in_specs=in_specs, out_specs=out_specs, check_vma=False)
```

```python
import functools

import jax
import jax.numpy as jnp
from jax import lax
from jax.experimental import pallas as pl
from jax.experimental.pallas import tpu as pltpu
from jax.sharding import PartitionSpec as P

SPECIAL = 4
TOK = 448
HALF = 224
D = 2304
W = 288
ZN = 16
SRC = 8
FEAT = 64

eps_rms = 1e-06
beta_one = 0.9
beta_two = 0.999
adam_count = 100.0
l1_coeff = 0.2

F32 = jnp.float32
BF16 = jnp.bfloat16


def tiles(v):
    return v.reshape(v.shape[0] // 16, 16, 128)


def rows(v):
    return v.reshape(v.shape[0] * 16, 128)


def dot(a, b, ca=1, cb=0):
    return lax.dot_general(a, b, (((ca,), (cb,)), ((), ())), preferred_element_type=F32)


def lane_group(shape):
    return lax.broadcasted_iota(jnp.int32, shape, len(shape) - 1)


def fold(read, lanes):
    out = read(3)
    for g in (2, 1, 0):
        out = jnp.where(lanes < 32 * (g + 1), read(g), out)
    return out


FAR = (8, 9, 7, 10, 6, 11, 5, 12, 4, 13, 3)
GROUPS = ((3, 5), (12, 14), (5, 7), (10, 12), (7, 8), (9, 10), (8, 9))
GROUP_OF = {place: g for g, (lo, hi) in enumerate(GROUPS) for place in range(lo, hi)}


def adam(grad, first, second, clip):
    corr_one = 1.0 - beta_one**adam_count
    corr_two = 1.0 - beta_two**adam_count
    scaled_grad = clip * grad
    mean = (beta_one / corr_one) * first.astype(F32) + ((1.0 - beta_one) / corr_one) * scaled_grad
    power = (beta_two / corr_two) * second.astype(F32) + ((1.0 - beta_two) / corr_two) * (scaled_grad * scaled_grad)
    return (mean / (jnp.sqrt(power) + 1e-08)).astype(BF16)


def adam_kernel(clip, eg, ef, es, dg, df, ds, eo_h, do_h, eo, do, sem):
    scale = clip[0:1, 0:1]
    copies = []
    for p in range(6):
        at = slice(384 * p, 384 * p + 384)
        do[:, at] = adam(dg[:, at], df[:, at], ds[:, at], scale)
        copies.append(pltpu.make_async_copy(do.at[:, at], do_h.at[:, at], sem.at[2 * p]))
        copies[-1].start()
        eo[at] = adam(eg[at], ef[at], es[at], scale)
        copies.append(pltpu.make_async_copy(eo.at[at], eo_h.at[at], sem.at[2 * p + 1]))
        copies[-1].start()
    for cp in copies:
        cp.wait()


def kernel(
    res_h, tok_h, gain_h, gw_h, uw_h, dw_h, ew_h, eb_h, dcw_h, db_h, ef_h, es_h, df_h, ds_h,
    eg, dg, clip, ef, es, df, ds,
    res_t, gain, gw, uw, tok, eb, db, dw, ew, dcw, ebx,
    rf, rn, rt, gu, p1r, sqs, sqr, hb, hh, dwf, tail, rest, ot, p3r,
    gs, ss, twb, bias, pa, lat_t, tt, p5r, zb, own, aa, p5z, ee, st,
    dgs, dgr, egs, egr, n7, n7z, n7x,
    lsem, wsend, wrecv, ssem, rsem,
):
    s = lax.axis_index("src")
    f = lax.axis_index("feat")
    c = lax.rem(f, 2)
    q = lax.div(f, 2)
    z = lax.rem(q, ZN)
    yhi = lax.div(q, ZN)
    xy = s * 2 + yhi
    half = lax.div(s, 4)

    def to(src, feat):
        return {"device_id": (src, feat), "device_id_type": pl.DeviceIdType.MESH}

    other = to(s, q * 2 + 1 - c)

    def src_peer(d, core):
        return to(lax.rem(s + d, SRC), q * 2 + core)

    def q_peer(d):
        return to(s, lax.rem(q + d, 32) * 2 + c)

    def z_peer(d):
        return to(s, (yhi * ZN + lax.rem(z + d, ZN)) * 2 + c)

    def xy_peer(d, core=c):
        i = lax.rem(xy + d, 16)
        return to(lax.div(i, 2), (lax.rem(i, 2) * ZN + z) * 2 + core)

    def loop(n, fn):
        def body(d, carry):
            fn(d)
            return carry

        lax.fori_loop(1, n, body, 0)

    def send(src, dst, k, where, at=None):
        pltpu.make_async_remote_copy(
            src_ref=src, dst_ref=dst, send_sem=ssem.at[k], recv_sem=rsem.at[k if at is None else at], **where
        ).start()

    def arrived(ref, k):
        pltpu.make_async_copy(ref, ref, rsem.at[k]).wait()

    def left(ref, k):
        pltpu.make_async_copy(ref, ref, ssem.at[k]).wait()

    place_of = [lax.rem(k + ZN - z, ZN) for k in range(ZN)]

    def far_first(n, d):
        step = lax.div(d, 2)
        return n // 2 + jnp.where(lax.rem(d, 2) == 0, step, -step)

    def gather(buf, k, m):
        mine = buf.at[xy, 0]
        for d in FAR:
            send(mine, buf.at[xy, ZN - d], k, z_peer(d), m + GROUP_OF[ZN - d])
        loop(16, lambda d: send(mine, mine, k + 1, xy_peer(d), m + 7))

        def onward(g):
            lo, hi = GROUPS[g]
            arrived(buf.at[0, lo:hi], m + g)
            part = buf.at[xy, lo:hi]
            loop(16, lambda d: send(part, part, k + 1, xy_peer(d), m + 8))

        onward(0)
        onward(1)
        arrived(buf.at[0, 0:15], m + 7)
        for d in (2, 14, 1, 15):
            send(buf.at[:, 0], buf.at[:, ZN - d], k + 2, z_peer(d), m + 9)
        onward(2)
        for g in (3, 4, 5, 6):
            onward(g)
        arrived(buf.at[0:15, 0:11], m + 8)
        arrived(buf.at[:, 0:4], m + 9)

    def gathered(buf, k):
        left(buf.at[0, 0:11], k)
        left(buf.at[0:15, 0:12], k + 1)
        left(buf.at[:, 0:4], k + 2)

    fetched = []
    for k, (src, dst) in enumerate(((res_h, res_t), (gain_h, gain), (gw_h, gw), (uw_h, uw), (tok_h, tok), (eb_h, eb), (db_h, db))):
        cp = pltpu.make_async_copy(src, dst, lsem.at[7 + k])
        cp.start()
        fetched.append(cp)

    barrier = pltpu.get_barrier_semaphore()

    def greet(where):
        pl.semaphore_signal(barrier, inc=1, **where)

    def greet_z(d):
        k = far_first(ZN, d)
        greet(q_peer(k))
        greet(q_peer(k + 16))

    def greet_src(d):
        k = far_first(SRC, d)
        greet(src_peer(k, c))
        greet(src_peer(k, 1 - c))
        for core in (c, 1 - c):
            greet(to(lax.rem(s + k, SRC), (lax.rem(yhi + 1, 2) * ZN + z) * 2 + core))

    loop(ZN, greet_z)
    loop(SRC, greet_src)
    greet(q_peer(16))
    greet(other)
    greet(to(s, (lax.rem(yhi + 1, 2) * ZN + z) * 2 + 1 - c))

    loads = []
    for k, (src, dst) in enumerate(
        ((dw_h, dw), (ew_h, ew.at[0]), (dcw_h, dcw.at[0]), (ef_h, ef), (es_h, es), (df_h, df), (ds_h, ds))
    ):
        cp = pltpu.make_async_copy(src, dst, lsem.at[k])
        cp.start()
        loads.append(cp)

    lanes = lane_group((64, 128))
    pick = jnp.where(
        jnp.bitwise_and(lane_group((32, 128)), 31) == lax.broadcasted_iota(jnp.int32, (32, 128), 0), 1.0, 0.0
    ).astype(BF16)

    tail[448:512] = jnp.zeros((64, 256), F32)
    fetched[0].wait()
    fetched[1].wait()
    rf[...] = jnp.concatenate([res_t[...], jnp.zeros((W, 64), BF16)], axis=1).T
    xg = (rf[0:448].astype(F32) * gain[...].astype(F32).reshape(1, W)).astype(BF16)
    fetched[2].wait()
    fetched[3].wait()
    spread = dot(jnp.concatenate([gw[:, 256:288], uw[:, 256:288]], axis=0), pick).astype(BF16)
    tail[0:448] = dot(xg, jnp.concatenate([spread[0:W], spread[W : 2 * W]], axis=1))
    for k, w in enumerate((gw, uw)):
        main = dot(xg, w[:, 0:256])
        for h in range(2):
            for j in range(2):
                gu[k, h * 32 + 14 * j : h * 32 + 14 * j + 14] = tiles(
                    main[224 * h : 224 * h + 224, 128 * j : 128 * j + 128].astype(BF16)
                )
            part = fold(
                lambda g: tail[224 * h + 64 * g : 224 * h + 64 * g + 64, 128 * k : 128 * k + 128], lanes
            )
            gu[k, h * 32 + 28 : h * 32 + 32] = tiles(part.astype(BF16))
    wide = res_t[...].astype(F32)
    squares = jnp.sum(wide * wide, axis=0, keepdims=True)
    squares = jnp.concatenate([squares, jnp.zeros((1, 64), F32)], axis=1)
    sqs[...] = jnp.concatenate(
        [squares[:, 128 * k : 128 * k + 128] for k in range(4)] + [jnp.zeros((4, 128), F32)], axis=0
    )

    pl.semaphore_wait(barrier, 61)

    def send_p1(d):
        k = far_first(SRC, d)
        send(sqs, sqr.at[k - 1], 1, src_peer(k, c))
        send(gu.at[:, pl.ds(8 * lax.rem(s + k, SRC), 8)], p1r.at[k - 1], 0, src_peer(k, c))

    loop(SRC, send_p1)

    for k in (4, 5, 6):
        fetched[k].wait()
    ids = tok[...]
    live = jnp.where(ids >= SPECIAL, 1.0, 0.0)
    weight = live / jnp.maximum(jnp.sum(live), 1.0)
    weight = jnp.concatenate([weight, jnp.zeros((1, 64), F32)], axis=1)
    weight = jnp.concatenate(
        [weight[:, 128 * k : 128 * k + 128] for k in range(4)] + [jnp.zeros((124, 128), F32)], axis=0
    ).T
    for k in range(4):
        twb[128 * k : 128 * k + 128] = jnp.broadcast_to(weight[:, k : k + 1], (128, 128))
    for k in range(18):
        bias[k] = jnp.broadcast_to(db[128 * k : 128 * k + 128].astype(F32).reshape(1, 128), (8, 128))
    ebx[0] = jnp.broadcast_to(eb[...].astype(F32), (8, 128))

    def share(ref, k):
        return pltpu.make_async_remote_copy(
            src_ref=ref.at[0], dst_ref=ref.at[1], send_sem=wsend.at[k], recv_sem=wrecv.at[k], **other
        )

    shares = [share(ebx, 0), share(dwf, 1), share(ew, 2), share(dcw, 3)]
    shares[0].start()
    loads[0].wait()
    spread = dot(dw[:, 256:288], pick).astype(BF16)
    dwf[0, 0:256, 0:256] = dw[0:256, 0:256]
    dwf[0, 0:256, 256:384] = spread[0:256]
    for g in range(4):
        dwf[0, 256 + 32 * g : 288 + 32 * g, 0:256] = dw[256:288, 0:256]
        dwf[0, 256 + 32 * g : 288 + 32 * g, 256:384] = spread[256:288]
    shares[1].start()
    loads[1].wait()
    shares[2].start()
    loads[2].wait()
    shares[3].start()

    off = pl.multiple_of(HALF * c, 32)
    for j in range(2):
        rest[14 * j : 14 * j + 14] = tiles(rf[pl.ds(off, HALF), 128 * j : 128 * j + 128].astype(F32))
    tail[:, 0:128] = dot(rf[:, 256:288], pick)
    rest[28:32] = tiles(fold(lambda g: tail[pl.ds(off + 64 * g, 64), 0:128], lanes))
    ss[252:256] = jnp.zeros((4, 16, 128), BF16)
    for k in range(12, 16):
        tt[15, place_of[k]] = jnp.zeros((16, 128), BF16)

    arrived(sqr, 1)
    total = sqs[...]
    for d in range(7):
        total = total + sqr[d]
    inv = lax.rsqrt(total / D + eps_rms)
    inv = jnp.concatenate([inv, jnp.zeros((120, 128), F32)], axis=0).T
    for k in range(4):
        rn[128 * k : 128 * k + 128] = jnp.broadcast_to(inv[:, k : k + 1], (128, 128))
    for h in range(2):
        for j in range(2):
            rt[h * 32 + 14 * j : h * 32 + 14 * j + 14] = tiles(rn[224 * h : 224 * h + 224])
        rt[h * 32 + 28 : h * 32 + 32] = tiles(
            fold(lambda g: rn[224 * h + 64 * g : 224 * h + 64 * g + 64], lanes)
        )

    arrived(p1r, 0)
    acts = []
    for k in range(2):
        acc = gu[k, pl.ds(8 * s, 8)].astype(F32)
        for d in range(7):
            acc = acc + p1r[d, k].astype(F32)
        acts.append(acc * rt[pl.ds(8 * s, 8)])
    hb[...] = (jax.nn.gelu(acts[0], approximate=True) * acts[1]).astype(BF16)

    slot = jnp.where(c == half, 0, 1)
    place = hh.at[slot, pl.ds(8 * lax.rem(s, 4), 8)]

    @pl.when(c == half)
    def _():
        pltpu.make_async_copy(hb, place, rsem.at[2]).start()

    @pl.when(c != half)
    def _():
        send(hb, place, 2, src_peer(0, half))

    loop(SRC, lambda d: send(hb, place, 2, src_peer(d, half)))
    shares[1].wait()
    arrived(hh, 2)
    acc = jnp.zeros((HALF, 384), F32)
    for k in range(2):
        last = rows(hh[k, 28:32])
        keep = jnp.zeros_like(last)
        split = jnp.concatenate(
            [jnp.where((lanes >= 32 * g) & (lanes < 32 * g + 32), last, keep) for g in range(4)], axis=0
        )[0:HALF]
        lhs = jnp.concatenate([rows(hh[k, 0:14]), rows(hh[k, 14:28]), split], axis=1)
        acc = acc + dot(lhs, dwf[k])
    for j in range(2):
        ot[14 * j : 14 * j + 14] = tiles(acc[:, 128 * j : 128 * j + 128].astype(BF16))
    tail[0:224, 0:128] = acc[:, 256:384]
    ot[28:32] = tiles(fold(lambda g: tail[64 * g : 64 * g + 64, 0:128], lanes).astype(BF16))


    def send_p3(d):
        k = far_first(ZN, d)
        send(ot.at[lax.rem(q + k, 32)], p3r.at[k - 1], 3, q_peer(k))
        send(ot.at[lax.rem(q + k + 16, 32)], p3r.at[k + 15], 3, q_peer(k + 16))

    loop(ZN, send_p3)
    send(ot.at[lax.rem(q + 16, 32)], p3r.at[15], 3, q_peer(16))
    arrived(p3r, 3)
    acc = ot[q].astype(F32)
    for d in range(31):
        acc = acc + p3r[d].astype(F32)
    gs[xy, 0] = (rest[q] + acc).astype(BF16)

    gather(gs, 4, 14)

    def picked(buf, first, n):
        return jnp.concatenate([buf[t // 16, place_of[t % 16]] for t in range(first, first + n)], axis=0)

    acc = jnp.zeros((HALF, 128), F32)
    rem = jnp.zeros((64, 128), F32)
    for k in range(SRC):
        for j in range(2):
            v = picked(gs, 32 * k + 14 * j, 14).astype(F32)
            acc = acc + v * v
        v = picked(gs, 32 * k + 28, 4).astype(F32)
        rem = rem + v * v
    acc = acc + jnp.concatenate(
        [jnp.where((lanes >= 32 * g) & (lanes < 32 * g + 32), rem, 0.0) for g in range(4)], axis=0
    )[0:HALF]
    inv = lax.rsqrt(jnp.sum(acc, axis=1, keepdims=True) / D + eps_rms)
    tall = lane_group((HALF, 128))

    def turn(v, by):
        by = by % 128
        return v if by == 0 else pltpu.roll(v, by, 1)

    for k in range(SRC):
        m, base = k % 4, 9 * (k // 4)
        a0 = turn(picked(gs, 32 * k, 14).astype(F32) * inv, 32 * m)
        a1 = turn(picked(gs, 32 * k + 14, 14).astype(F32) * inv, 32 * m)
        last = picked(gs, 32 * k + 28, 4).astype(F32)
        rem = jnp.concatenate([turn(last, 32 * m - 32 * g) for g in range(4)], axis=0)[0:HALF] * inv
        if m == 0:
            first, second = a0, a1
        else:
            first = jnp.where(tall < 32 * m, carry, a0)
            second = jnp.where(tall < 32 * m, a0, a1)
        carry = jnp.where(tall < 32 * m, a1, rem)
        for at, v in ((2 * m, first), (2 * m + 1, second)) + (((8, carry),) if m == 3 else ()):
            ss[14 * (base + at) : 14 * (base + at) + 14] = tiles(v.astype(BF16))

    def cols_of(ref, p):
        return jnp.concatenate([rows(ref[28 * p : 28 * p + 14]), rows(ref[28 * p + 14 : 28 * p + 28])], axis=1)

    for k in (0, 2, 3):
        shares[k].wait()
    acc = jnp.zeros((HALF, 256), F32)
    for p in range(9):
        rhs = jnp.concatenate([ew[0, 256 * p : 256 * p + 256], ew[1, 256 * p : 256 * p + 256]], axis=1)
        acc = acc + dot(cols_of(ss, p), rhs)
    acc = acc + jnp.concatenate([ebx[0, 0:1], ebx[1, 0:1]], axis=1)
    pa[...] = acc
    latents = jnp.maximum(acc, 0.0)
    lat = latents.astype(BF16)
    for p in range(9):
        rhs = jnp.concatenate([dcw[0, :, 256 * p : 256 * p + 256], dcw[1, :, 256 * p : 256 * p + 256]], axis=0)
        r = dot(lat, rhs).astype(BF16)
        for t in range(28 * p, 28 * p + 28):
            k = t - 28 * p
            tt[t // 16, place_of[t % 16]] = r[16 * (k % 14) : 16 * (k % 14) + 16, 128 * (k // 14) : 128 * (k // 14) + 128]

    def across(g):
        lo, hi = GROUPS[g]
        loop(
            16,
            lambda d: send(
                tt.at[lax.rem(xy + d, 16), lo:hi], p5r.at[d - 1, lo:hi], 7, xy_peer(d), 24 + g
            ),
        )

    for g in (6, 4, 5):
        across(g)
    for k, d in enumerate((2, 14, 1, 15)):
        send(tt.at[:, d], zb.at[k], 8, z_peer(d), 31)
    for g in (2, 3, 0, 1):
        across(g)
    lat_t[...] = jnp.concatenate([latents, jnp.zeros((32, 256), F32)], axis=0).T.astype(BF16)
    for p in range(18):
        v = rows(ss[14 * p : 14 * p + 14]).astype(F32)
        st[128 * p : 128 * p + 128] = jnp.concatenate([v, jnp.zeros((32, 128), F32)], axis=0).T.astype(BF16)

    def onward(g):
        lo, hi = GROUPS[g]
        arrived(p5r.at[:, lo:hi], 24 + g)
        for k in range(lo, hi):
            acc = tt[xy, k].astype(F32)
            for d in range(15):
                acc = acc + p5r[d, k].astype(F32)
            aa[k] = acc.astype(BF16)
            send(aa.at[k], p5z.at[k - 3], 9, z_peer(k), 33)

    for g in (6, 4, 5):
        onward(g)
    arrived(zb, 31)
    for k in range(16):
        acc = tt[k, 0].astype(F32)
        for d in range(4):
            acc = acc + zb[d, k].astype(F32)
        own[k] = acc.astype(BF16)
    loop(16, lambda d: send(own.at[lax.rem(xy + d, 16)], p5r.at[d - 1, 0], 7, xy_peer(d), 32))
    for g in (2, 3, 0, 1):
        onward(g)
    arrived(p5r.at[:, 0], 32)
    acc = own[xy].astype(F32)
    for d in range(15):
        acc = acc + p5r[d, 0].astype(F32)
    arrived(p5z, 33)
    for d in range(11):
        acc = acc + p5z[d].astype(F32)
    t = xy * 16 + z
    col = jnp.minimum(lax.div(t, 14), 17)
    row = lax.rem(t, 14)
    err = (acc + bias[col, 0:1] - ss[t].astype(F32)).astype(BF16)
    tw = twb[pl.ds(pl.multiple_of(off + 16 * row, 16), 16)]
    ee[xy, 0] = (2.0 * tw * err.astype(F32)).astype(BF16)
    gather(ee, 10, 34)

    def err_cols(p):
        return jnp.concatenate([picked(ee, 28 * p, 14), picked(ee, 28 * p + 14, 14)], axis=1)

    acc = jnp.zeros((HALF, 256), F32)
    for p in range(9):
        rhs = jnp.concatenate([dcw[0, :, 256 * p : 256 * p + 256], dcw[1, :, 256 * p : 256 * p + 256]], axis=0)
        acc = acc + dot(err_cols(p), rhs, 1, 1)
    tw = l1_coeff * twb[pl.ds(off, HALF)]
    acc = acc + jnp.concatenate([tw, tw], axis=1)
    pg = jnp.where(pa[...] > 0.0, acc, 0.0).astype(BF16)
    for p in range(9):
        r = dot(st[256 * p : 256 * p + 256, 0:HALF], pg)
        eg[256 * p : 256 * p + 256] = r[:, 0:128]
        egs[256 * p : 256 * p + 256] = r[:, 128:256].astype(BF16)
        if p % 3 == 2:
            part = pl.ds(768 * (p // 3), 768)
            send(egs.at[part], egr.at[part], 13, other, 44 + p // 3)
    lt = lat_t[:, 0:HALF]
    for p in range(9):
        r = dot(lt, err_cols(p))
        dg[:, 256 * p : 256 * p + 256] = r[0:128]
        dgs[:, 256 * p : 256 * p + 256] = r[128:256].astype(BF16)
        if p % 3 == 2:
            part = pl.ds(768 * (p // 3), 768)
            send(dgs.at[:, part], dgr.at[:, part], 14, other, 47 + p // 3)
    acc = jnp.zeros((8, 128), F32)
    for p in range(18):
        if p % 6 == 0:
            arrived(egr.at[0:768], 44 + p // 6)
        v = eg[128 * p : 128 * p + 128] + egr[128 * p : 128 * p + 128].astype(F32)
        eg[128 * p : 128 * p + 128] = v
        acc = acc + jnp.sum((v * v).reshape(16, 8, 128), axis=0)
    for p in range(18):
        if p % 6 == 0:
            arrived(dgr.at[:, 0:768], 47 + p // 6)
        v = dg[:, 128 * p : 128 * p + 128] + dgr[:, 128 * p : 128 * p + 128].astype(F32)
        dg[:, 128 * p : 128 * p + 128] = v
        acc = acc + jnp.sum((v * v).reshape(16, 8, 128), axis=0)

    n7[0] = acc

    def send_n(d):
        k = far_first(ZN, d)
        send(n7.at[0], n7z.at[k - 1], 15, z_peer(k), 50)

    loop(ZN, send_n)
    arrived(n7z, 50)
    for d in range(15):
        acc = acc + n7z[d]
    n7[1] = acc

    def send_xy(d):
        send(n7.at[1], n7x.at[d - 1], 16, xy_peer(d), 51)
        send(n7.at[1], n7x.at[d + 15], 16, xy_peer(d, 1 - c), 51)

    loop(16, send_xy)
    send(n7.at[1], n7x.at[15], 16, other, 51)
    arrived(n7x, 51)
    for d in range(31):
        acc = acc + n7x[d]
    clip[...] = jnp.broadcast_to(lax.rsqrt(jnp.sum(acc, keepdims=True) + 1e-12), (8, 128))
    for k in range(3, 7):
        loads[k].wait()

    left(p1r, 0)
    left(sqr, 1)

    @pl.when(c == half)
    def _():
        left(hh.at[0, 0:28], 2)
        left(hh.at[1, 0:28], 2)

    @pl.when(c != half)
    def _():
        left(hh, 2)

    left(p3r, 3)
    gathered(gs, 4)
    left(p5r.at[:, 0:12], 7)
    left(zb, 8)
    left(p5z, 9)
    gathered(ee, 10)
    left(egs, 13)
    left(dgs, 14)
    left(n7z, 15)
    left(n7x, 16)


def local(
    residual, token_ids, ffn_gain, gate_w, up_w, down_w, enc_w, enc_bias, dec_w, dec_bias,
    enc_first, enc_second, dec_first, dec_second,
):
    vm = pl.BlockSpec(memory_space=pltpu.VMEM)
    hbm = pl.BlockSpec(memory_space=pl.ANY)
    V = pltpu.VMEM
    scratch = [
        V((W, TOK), BF16), V((W,), BF16), V((W, W), BF16), V((W, W), BF16), V((1, TOK), jnp.int32),
        V((1, 128), BF16), V((D,), BF16), V((W, W), BF16), V((2, D, 128), BF16), V((2, 128, D), BF16), V((2, 8, 128), F32),
        V((512, W), BF16), V((512, 128), F32), V((64, 16, 128), F32), V((2, 64, 16, 128), BF16),
        V((7, 2, 8, 16, 128), BF16), V((8, 128), F32), V((7, 8, 128), F32), V((8, 16, 128), BF16),
        V((2, 32, 16, 128), BF16), V((2, 384, 384), BF16), V((512, 256), F32), V((32, 16, 128), F32),
        V((32, 16, 128), BF16), V((31, 16, 128), BF16),
        V((16, 16, 16, 128), BF16), V((256, 16, 128), BF16), V((512, 128), F32), V((18, 8, 128), F32),
        V((HALF, 256), F32), V((256, 256), BF16), V((16, 16, 16, 128), BF16), V((15, 16, 16, 128), BF16),
        V((4, 16, 16, 128), BF16), V((16, 16, 128), BF16), V((16, 16, 128), BF16), V((11, 16, 128), BF16),
        V((16, 16, 16, 128), BF16), V((D, 256), BF16),
        V((128, D), BF16), V((128, D), BF16), V((D, 128), BF16), V((D, 128), BF16),
        V((2, 8, 128), F32), V((15, 8, 128), F32), V((31, 8, 128), F32),
        pltpu.SemaphoreType.DMA((14,)), pltpu.SemaphoreType.DMA((4,)), pltpu.SemaphoreType.DMA((4,)),
        pltpu.SemaphoreType.DMA((17,)), pltpu.SemaphoreType.DMA((52,)),
    ]
    operands = [
        pltpu.with_memory_space_constraint(v, pltpu.HBM)
        for v in (
            residual.T, token_ids.reshape(1, TOK), ffn_gain, gate_w, up_w, down_w, enc_w,
            enc_bias.reshape(1, 128), dec_w, dec_bias, enc_first, enc_second, dec_first, dec_second,
        )
    ]
    tall, flat = jax.ShapeDtypeStruct((D, 128), BF16), jax.ShapeDtypeStruct((128, D), BF16)
    enc_grad, dec_grad, clip, enc_one, enc_two, dec_one, dec_two = pl.pallas_call(
        kernel,
        out_shape=(
            jax.ShapeDtypeStruct((D, 128), F32),
            jax.ShapeDtypeStruct((128, D), F32),
            jax.ShapeDtypeStruct((8, 128), F32),
            tall, tall, flat, flat,
        ),
        in_specs=[hbm] * 14,
        out_specs=(vm,) * 7,
        scratch_shapes=scratch,
        compiler_params=pltpu.CompilerParams(
            collective_id=0, has_side_effects=True, vmem_limit_bytes=32 << 20
        ),
    )(*operands)
    return pl.pallas_call(
        adam_kernel,
        out_shape=(tall, flat),
        in_specs=[vm] * 7,
        out_specs=(hbm, hbm),
        scratch_shapes=[V((D, 128), BF16), V((128, D), BF16), pltpu.SemaphoreType.DMA((12,))],
        compiler_params=pltpu.CompilerParams(vmem_limit_bytes=16 << 20),
    )(clip, enc_grad, enc_one, enc_two, dec_grad, dec_one, dec_two)


def solution(mesh):
    in_specs = (
        P(None, "src"),
        P(),
        P("src"),
        P("src", "feat"),
        P("src", "feat"),
        P("feat", "src"),
        P(None, ("src", "feat")),
        P(("src", "feat")),
        P(("src", "feat"), None),
        P(),
        P(None, ("src", "feat")),
        P(None, ("src", "feat")),
        P(("src", "feat"), None),
        P(("src", "feat"), None),
    )
    out_specs = (P(None, ("src", "feat")), P(("src", "feat"), None))
    return jax.shard_map(local, mesh=mesh, in_specs=in_specs, out_specs=out_specs, check_vma=False)
```

```python
import functools

import jax
import jax.numpy as jnp
from jax import lax
from jax.experimental import pallas as pl
from jax.experimental.pallas import tpu as pltpu
from jax.sharding import PartitionSpec as P

SPECIAL = 4
TOK = 448
HALF = 224
D = 2304
W = 288
ZN = 16
SRC = 8
FEAT = 64

eps_rms = 1e-06
beta_one = 0.9
beta_two = 0.999
adam_count = 100.0
l1_coeff = 0.2

F32 = jnp.float32
BF16 = jnp.bfloat16


def tiles(v):
    return v.reshape(v.shape[0] // 16, 16, 128)


def rows(v):
    return v.reshape(v.shape[0] * 16, 128)


def dot(a, b, ca=1, cb=0):
    return lax.dot_general(a, b, (((ca,), (cb,)), ((), ())), preferred_element_type=F32)


def lane_group(shape):
    return lax.broadcasted_iota(jnp.int32, shape, len(shape) - 1)


def fold(read, lanes):
    out = read(3)
    for g in (2, 1, 0):
        out = jnp.where(lanes < 32 * (g + 1), read(g), out)
    return out


FAR = (8, 9, 7, 10, 6, 11, 5, 12, 4, 13, 3)
GROUPS = ((3, 5), (12, 14), (5, 7), (10, 12), (7, 8), (9, 10), (8, 9))
GROUP_OF = {place: g for g, (lo, hi) in enumerate(GROUPS) for place in range(lo, hi)}


def adam(grad, first, second, clip):
    corr_one = 1.0 - beta_one**adam_count
    corr_two = 1.0 - beta_two**adam_count
    scaled_grad = clip * grad
    mean = (beta_one / corr_one) * first.astype(F32) + ((1.0 - beta_one) / corr_one) * scaled_grad
    power = (beta_two / corr_two) * second.astype(F32) + ((1.0 - beta_two) / corr_two) * (scaled_grad * scaled_grad)
    return (mean / (jnp.sqrt(power) + 1e-08)).astype(BF16)


def adam_kernel(clip, eg, ef, es, dg, df, ds, eo_h, do_h, eo, do, sem):
    scale = clip[0:1, 0:1]
    copies = []
    for p in range(6):
        at = slice(384 * p, 384 * p + 384)
        do[:, at] = adam(dg[:, at], df[:, at], ds[:, at], scale)
        copies.append(pltpu.make_async_copy(do.at[:, at], do_h.at[:, at], sem.at[2 * p]))
        copies[-1].start()
        eo[at] = adam(eg[at], ef[at], es[at], scale)
        copies.append(pltpu.make_async_copy(eo.at[at], eo_h.at[at], sem.at[2 * p + 1]))
        copies[-1].start()
    for cp in copies:
        cp.wait()


def kernel(
    res_h, tok_h, gain_h, gw_h, uw_h, dw_h, ew_h, eb_h, dcw_h, db_h, ef_h, es_h, df_h, ds_h,
    eg, dg, clip, ef, es, df, ds,
    res_t, gain, gw, uw, tok, eb, db, dw, ew, dcw, ebx,
    rf, rn, rt, gu, p1r, sqs, sqr, hb, hh, dwf, tail, rest, ot, p3r,
    gs, ss, twb, bias, pa, lat_t, tt, p5r, zb, own, aa, p5z, ee, st,
    dgs, dgr, egs, egr, n7, n7z, n7x,
    lsem, wsend, wrecv, ssem, rsem,
):
    s = lax.axis_index("src")
    f = lax.axis_index("feat")
    c = lax.rem(f, 2)
    q = lax.div(f, 2)
    z = lax.rem(q, ZN)
    yhi = lax.div(q, ZN)
    xy = s * 2 + yhi
    half = lax.div(s, 4)
    x = lax.div(s, 2)
    y = lax.rem(s, 2) * 2 + yhi

    def to(src, feat):
        return {"device_id": (src, feat), "device_id_type": pl.DeviceIdType.MESH}

    other = to(s, q * 2 + 1 - c)

    def src_peer(d, core):
        return to(lax.rem(s + d, SRC), q * 2 + core)

    def q_peer(d):
        return to(s, lax.rem(q + d, 32) * 2 + c)

    def z_peer(d):
        return to(s, (yhi * ZN + lax.rem(z + d, ZN)) * 2 + c)

    def xy_peer(d, core=c):
        i = lax.rem(xy + d, 16)
        return to(lax.div(i, 2), (lax.rem(i, 2) * ZN + z) * 2 + core)

    def x_peer(d):
        return to(lax.rem(x + d, 4) * 2 + lax.div(y, 2), f)

    def y_peer(d):
        k = lax.rem(y + d, 4)
        return to(x * 2 + lax.div(k, 2), (lax.rem(k, 2) * ZN + z) * 2 + c)

    def loop(n, fn):
        def body(d, carry):
            fn(d)
            return carry

        lax.fori_loop(1, n, body, 0)

    def send(src, dst, k, where, at=None):
        pltpu.make_async_remote_copy(
            src_ref=src, dst_ref=dst, send_sem=ssem.at[k], recv_sem=rsem.at[k if at is None else at], **where
        ).start()

    def arrived(ref, k):
        pltpu.make_async_copy(ref, ref, rsem.at[k]).wait()

    def left(ref, k):
        pltpu.make_async_copy(ref, ref, ssem.at[k]).wait()

    place_of = [lax.rem(k + ZN - z, ZN) for k in range(ZN)]

    def far_first(n, d):
        step = lax.div(d, 2)
        return n // 2 + jnp.where(lax.rem(d, 2) == 0, step, -step)

    def gather(buf, k, m):
        mine = buf.at[x, y, 0]
        for d in FAR:
            send(mine, buf.at[x, y, ZN - d], k, z_peer(d), m + GROUP_OF[ZN - d])
        loop(16, lambda d: send(mine, mine, k + 1, xy_peer(d), m + 7))

        def first(g):
            lo, hi = GROUPS[g]
            arrived(buf.at[0, 0, lo:hi], m + g)
            part = buf.at[x, y, lo:hi]
            for d in (2, 1, 3):
                send(part, part, k + 3, x_peer(d) if g % 2 == 0 else y_peer(d), m + 10 + g)

        def second(g):
            lo, hi = GROUPS[g]
            arrived(buf.at[0:3, 0, lo:hi], m + 10 + g)
            part = buf.at[:, y, lo:hi] if g % 2 == 0 else buf.at[x, :, lo:hi]
            for d in (2, 1, 3):
                send(part, part, k + 4, y_peer(d) if g % 2 == 0 else x_peer(d), m + 14)

        def direct(g):
            lo, hi = GROUPS[g]
            arrived(buf.at[0, 0, lo:hi], m + g)
            part = buf.at[x, y, lo:hi]
            loop(16, lambda d: send(part, part, k + 1, xy_peer(d), m + 8))

        first(0)
        first(1)
        arrived(buf.at[0, 0, 0:15], m + 7)
        for d in (2, 14, 1, 15):
            send(buf.at[:, :, 0], buf.at[:, :, ZN - d], k + 2, z_peer(d), m + 9)
        first(2)
        first(3)
        for g in (4, 5, 6):
            direct(g)
        for g in (0, 1, 2, 3):
            second(g)
        arrived(buf.at[0:3, 0:3, 0:5], m + 8)
        arrived(buf.at[0:3, :, 0:8], m + 14)
        arrived(buf.at[:, :, 0:4], m + 9)

    def gathered(buf, k):
        left(buf.at[0, 0, 0:11], k)
        left(buf.at[0:3, :, 0:5], k + 1)
        left(buf.at[:, :, 0:4], k + 2)
        left(buf.at[0:3, 0, 0:8], k + 3)
        left(buf.at[0:3, :, 0:8], k + 4)

    fetched = []
    for k, (src, dst) in enumerate(((res_h, res_t), (gain_h, gain), (gw_h, gw), (uw_h, uw), (tok_h, tok), (eb_h, eb), (db_h, db))):
        cp = pltpu.make_async_copy(src, dst, lsem.at[7 + k])
        cp.start()
        fetched.append(cp)

    barrier = pltpu.get_barrier_semaphore()

    def greet(where):
        pl.semaphore_signal(barrier, inc=1, **where)

    def greet_z(d):
        k = far_first(ZN, d)
        greet(q_peer(k))
        greet(q_peer(k + 16))

    def greet_src(d):
        k = far_first(SRC, d)
        greet(src_peer(k, c))
        greet(src_peer(k, 1 - c))
        for core in (c, 1 - c):
            greet(to(lax.rem(s + k, SRC), (lax.rem(yhi + 1, 2) * ZN + z) * 2 + core))

    loop(ZN, greet_z)
    loop(SRC, greet_src)
    greet(q_peer(16))
    greet(other)
    greet(to(s, (lax.rem(yhi + 1, 2) * ZN + z) * 2 + 1 - c))

    loads = []
    for k, (src, dst) in enumerate(
        ((dw_h, dw), (ew_h, ew.at[0]), (dcw_h, dcw.at[0]), (ef_h, ef), (es_h, es), (df_h, df), (ds_h, ds))
    ):
        cp = pltpu.make_async_copy(src, dst, lsem.at[k])
        cp.start()
        loads.append(cp)

    lanes = lane_group((64, 128))
    pick = jnp.where(
        jnp.bitwise_and(lane_group((32, 128)), 31) == lax.broadcasted_iota(jnp.int32, (32, 128), 0), 1.0, 0.0
    ).astype(BF16)

    tail[448:512] = jnp.zeros((64, 256), F32)
    fetched[0].wait()
    fetched[1].wait()
    rf[...] = jnp.concatenate([res_t[...], jnp.zeros((W, 64), BF16)], axis=1).T
    xg = (rf[0:448].astype(F32) * gain[...].astype(F32).reshape(1, W)).astype(BF16)
    fetched[2].wait()
    fetched[3].wait()
    spread = dot(jnp.concatenate([gw[:, 256:288], uw[:, 256:288]], axis=0), pick).astype(BF16)
    tail[0:448] = dot(xg, jnp.concatenate([spread[0:W], spread[W : 2 * W]], axis=1))
    for k, w in enumerate((gw, uw)):
        main = dot(xg, w[:, 0:256])
        for h in range(2):
            for j in range(2):
                gu[k, h * 32 + 14 * j : h * 32 + 14 * j + 14] = tiles(
                    main[224 * h : 224 * h + 224, 128 * j : 128 * j + 128].astype(BF16)
                )
            part = fold(
                lambda g: tail[224 * h + 64 * g : 224 * h + 64 * g + 64, 128 * k : 128 * k + 128], lanes
            )
            gu[k, h * 32 + 28 : h * 32 + 32] = tiles(part.astype(BF16))
    wide = res_t[...].astype(F32)
    squares = jnp.sum(wide * wide, axis=0, keepdims=True)
    squares = jnp.concatenate([squares, jnp.zeros((1, 64), F32)], axis=1)
    sqs[...] = jnp.concatenate(
        [squares[:, 128 * k : 128 * k + 128] for k in range(4)] + [jnp.zeros((4, 128), F32)], axis=0
    )

    pl.semaphore_wait(barrier, 61)

    def send_p1(d):
        k = far_first(SRC, d)
        send(sqs, sqr.at[k - 1], 1, src_peer(k, c))
        send(gu.at[:, pl.ds(8 * lax.rem(s + k, SRC), 4)], p1r.at[k - 1, :, 0:4], 0, src_peer(k, c))

    def send_p1_rest(d):
        k = far_first(SRC, d)
        send(gu.at[:, pl.ds(8 * lax.rem(s + k, SRC) + 4, 4)], p1r.at[k - 1, :, 4:8], 0, src_peer(k, c), 82)

    loop(SRC, send_p1)
    loop(SRC, send_p1_rest)

    for k in (4, 5, 6):
        fetched[k].wait()
    ids = tok[...]
    live = jnp.where(ids >= SPECIAL, 1.0, 0.0)
    weight = live / jnp.maximum(jnp.sum(live), 1.0)
    weight = jnp.concatenate([weight, jnp.zeros((1, 64), F32)], axis=1)
    weight = jnp.concatenate(
        [weight[:, 128 * k : 128 * k + 128] for k in range(4)] + [jnp.zeros((124, 128), F32)], axis=0
    ).T
    for k in range(4):
        twb[128 * k : 128 * k + 128] = jnp.broadcast_to(weight[:, k : k + 1], (128, 128))
    for k in range(18):
        bias[k] = jnp.broadcast_to(db[128 * k : 128 * k + 128].astype(F32).reshape(1, 128), (8, 128))
    ebx[0] = jnp.broadcast_to(eb[...].astype(F32), (8, 128))

    def share(ref, k):
        return pltpu.make_async_remote_copy(
            src_ref=ref.at[0], dst_ref=ref.at[1], send_sem=wsend.at[k], recv_sem=wrecv.at[k], **other
        )

    shares = [share(ebx, 0), share(dwf, 1), share(ew, 2), share(dcw, 3)]
    shares[0].start()
    loads[0].wait()
    spread = dot(dw[:, 256:288], pick).astype(BF16)
    dwf[0, 0:256, 0:256] = dw[0:256, 0:256]
    dwf[0, 0:256, 256:384] = spread[0:256]
    for g in range(4):
        dwf[0, 256 + 32 * g : 288 + 32 * g, 0:256] = dw[256:288, 0:256]
        dwf[0, 256 + 32 * g : 288 + 32 * g, 256:384] = spread[256:288]
    shares[1].start()
    loads[1].wait()
    shares[2].start()
    loads[2].wait()
    shares[3].start()

    off = pl.multiple_of(HALF * c, 32)
    for j in range(2):
        rest[14 * j : 14 * j + 14] = tiles(rf[pl.ds(off, HALF), 128 * j : 128 * j + 128].astype(F32))
    tail[:, 0:128] = dot(rf[:, 256:288], pick)
    rest[28:32] = tiles(fold(lambda g: tail[pl.ds(off + 64 * g, 64), 0:128], lanes))
    ss[252:256] = jnp.zeros((4, 16, 128), BF16)
    for k in range(12, 16):
        tt[15, place_of[k]] = jnp.zeros((16, 128), BF16)

    arrived(sqr, 1)
    total = sqs[...]
    for d in range(7):
        total = total + sqr[d]
    inv = lax.rsqrt(total / D + eps_rms)
    inv = jnp.concatenate([inv, jnp.zeros((120, 128), F32)], axis=0).T
    for k in range(4):
        rn[128 * k : 128 * k + 128] = jnp.broadcast_to(inv[:, k : k + 1], (128, 128))
    for h in range(2):
        for j in range(2):
            rt[h * 32 + 14 * j : h * 32 + 14 * j + 14] = tiles(rn[224 * h : 224 * h + 224])
        rt[h * 32 + 28 : h * 32 + 32] = tiles(
            fold(lambda g: rn[224 * h + 64 * g : 224 * h + 64 * g + 64], lanes)
        )

    slot = jnp.where(c == half, 0, 1)
    for n in range(2):
        at = slice(4 * n, 4 * n + 4)
        arrived(p1r.at[:, :, at], 82 * n)
        acts = []
        for k in range(2):
            acc = gu[k, pl.ds(8 * s + 4 * n, 4)].astype(F32)
            for d in range(7):
                acc = acc + p1r[d, k, at].astype(F32)
            acts.append(acc * rt[pl.ds(8 * s + 4 * n, 4)])
        hb[at] = (jax.nn.gelu(acts[0], approximate=True) * acts[1]).astype(BF16)
        ours = hb.at[at]
        place = hh.at[slot, pl.ds(8 * lax.rem(s, 4) + 4 * n, 4)]

        @pl.when(c == half)
        def _():
            pltpu.make_async_copy(ours, place, rsem.at[2]).start()

        @pl.when(c != half)
        def _():
            send(ours, place, 2, src_peer(0, half))

        loop(SRC, lambda d: send(ours, place, 2, src_peer(d, half)))
    shares[1].wait()
    arrived(hh, 2)
    acc = jnp.zeros((HALF, 384), F32)
    for k in range(2):
        last = rows(hh[k, 28:32])
        keep = jnp.zeros_like(last)
        split = jnp.concatenate(
            [jnp.where((lanes >= 32 * g) & (lanes < 32 * g + 32), last, keep) for g in range(4)], axis=0
        )[0:HALF]
        lhs = jnp.concatenate([rows(hh[k, 0:14]), rows(hh[k, 14:28]), split], axis=1)
        acc = acc + dot(lhs, dwf[k])
    for j in range(2):
        ot[14 * j : 14 * j + 14] = tiles(acc[:, 128 * j : 128 * j + 128].astype(BF16))
    tail[0:224, 0:128] = acc[:, 256:384]
    ot[28:32] = tiles(fold(lambda g: tail[64 * g : 64 * g + 64, 0:128], lanes).astype(BF16))


    def send_p3(d):
        k = far_first(ZN, d)
        send(ot.at[lax.rem(q + k, 32)], p3r.at[k - 1], 3, q_peer(k))
        send(ot.at[lax.rem(q + k + 16, 32)], p3r.at[k + 15], 3, q_peer(k + 16))

    loop(ZN, send_p3)
    send(ot.at[lax.rem(q + 16, 32)], p3r.at[15], 3, q_peer(16))
    arrived(p3r, 3)
    acc = ot[q].astype(F32)
    for d in range(31):
        acc = acc + p3r[d].astype(F32)
    gs[x, y, 0] = (rest[q] + acc).astype(BF16)

    gather(gs, 17, 52)

    def picked(buf, first, n):
        return jnp.concatenate([buf[t // 64, t // 16 % 4, place_of[t % 16]] for t in range(first, first + n)], axis=0)

    acc = jnp.zeros((HALF, 128), F32)
    rem = jnp.zeros((64, 128), F32)
    for k in range(SRC):
        for j in range(2):
            v = picked(gs, 32 * k + 14 * j, 14).astype(F32)
            acc = acc + v * v
        v = picked(gs, 32 * k + 28, 4).astype(F32)
        rem = rem + v * v
    acc = acc + jnp.concatenate(
        [jnp.where((lanes >= 32 * g) & (lanes < 32 * g + 32), rem, 0.0) for g in range(4)], axis=0
    )[0:HALF]
    inv = lax.rsqrt(jnp.sum(acc, axis=1, keepdims=True) / D + eps_rms)
    tall = lane_group((HALF, 128))

    def turn(v, by):
        by = by % 128
        return v if by == 0 else pltpu.roll(v, by, 1)

    for k in range(SRC):
        m, base = k % 4, 9 * (k // 4)
        a0 = turn(picked(gs, 32 * k, 14).astype(F32) * inv, 32 * m)
        a1 = turn(picked(gs, 32 * k + 14, 14).astype(F32) * inv, 32 * m)
        last = picked(gs, 32 * k + 28, 4).astype(F32)
        rem = jnp.concatenate([turn(last, 32 * m - 32 * g) for g in range(4)], axis=0)[0:HALF] * inv
        if m == 0:
            first, second = a0, a1
        else:
            first = jnp.where(tall < 32 * m, carry, a0)
            second = jnp.where(tall < 32 * m, a0, a1)
        carry = jnp.where(tall < 32 * m, a1, rem)
        for at, v in ((2 * m, first), (2 * m + 1, second)) + (((8, carry),) if m == 3 else ()):
            ss[14 * (base + at) : 14 * (base + at) + 14] = tiles(v.astype(BF16))

    def cols_of(ref, p):
        return jnp.concatenate([rows(ref[28 * p : 28 * p + 14]), rows(ref[28 * p + 14 : 28 * p + 28])], axis=1)

    for k in (0, 2, 3):
        shares[k].wait()
    acc = jnp.zeros((HALF, 256), F32)
    for p in range(9):
        rhs = jnp.concatenate([ew[0, 256 * p : 256 * p + 256], ew[1, 256 * p : 256 * p + 256]], axis=1)
        acc = acc + dot(cols_of(ss, p), rhs)
    acc = acc + jnp.concatenate([ebx[0, 0:1], ebx[1, 0:1]], axis=1)
    pa[...] = acc
    latents = jnp.maximum(acc, 0.0)
    lat = latents.astype(BF16)
    for p in range(9):
        rhs = jnp.concatenate([dcw[0, :, 256 * p : 256 * p + 256], dcw[1, :, 256 * p : 256 * p + 256]], axis=0)
        r = dot(lat, rhs).astype(BF16)
        for t in range(28 * p, 28 * p + 28):
            k = t - 28 * p
            tt[t // 16, place_of[t % 16]] = r[16 * (k % 14) : 16 * (k % 14) + 16, 128 * (k // 14) : 128 * (k // 14) + 128]

    def across(g):
        lo, hi = GROUPS[g]
        loop(
            16,
            lambda d: send(
                tt.at[lax.rem(xy + d, 16), lo:hi], p5r.at[d - 1, lo:hi], 7, xy_peer(d), 24 + g
            ),
        )

    for k, d in enumerate((2, 14, 1, 15)):
        send(tt.at[:, d], zb.at[k], 8, z_peer(d), 31)
    for g in (6, 4, 5):
        across(g)
    for g in (2, 3, 0, 1):
        across(g)
    lat_t[...] = jnp.concatenate([latents, jnp.zeros((32, 256), F32)], axis=0).T.astype(BF16)
    for p in range(18):
        v = rows(ss[14 * p : 14 * p + 14]).astype(F32)
        st[128 * p : 128 * p + 128] = jnp.concatenate([v, jnp.zeros((32, 128), F32)], axis=0).T.astype(BF16)

    def onward(g):
        lo, hi = GROUPS[g]
        arrived(p5r.at[:, lo:hi], 24 + g)
        for k in range(lo, hi):
            acc = tt[xy, k].astype(F32)
            for d in range(15):
                acc = acc + p5r[d, k].astype(F32)
            aa[k] = acc.astype(BF16)
            send(aa.at[k], p5z.at[k - 3], 9, z_peer(k), 33)

    for g in (6, 4, 5):
        onward(g)
    arrived(zb, 31)
    for k in range(16):
        acc = tt[k, 0].astype(F32)
        for d in range(4):
            acc = acc + zb[d, k].astype(F32)
        own[k] = acc.astype(BF16)
    loop(16, lambda d: send(own.at[lax.rem(xy + d, 16)], p5r.at[d - 1, 0], 7, xy_peer(d), 32))
    for g in (2, 3, 0, 1):
        onward(g)
    arrived(p5r.at[:, 0], 32)
    acc = own[xy].astype(F32)
    for d in range(15):
        acc = acc + p5r[d, 0].astype(F32)
    arrived(p5z, 33)
    for d in range(11):
        acc = acc + p5z[d].astype(F32)
    t = xy * 16 + z
    col = jnp.minimum(lax.div(t, 14), 17)
    row = lax.rem(t, 14)
    err = (acc + bias[col, 0:1] - ss[t].astype(F32)).astype(BF16)
    tw = twb[pl.ds(pl.multiple_of(off + 16 * row, 16), 16)]
    ee[x, y, 0] = (2.0 * tw * err.astype(F32)).astype(BF16)
    gather(ee, 22, 67)

    def err_cols(p):
        return jnp.concatenate([picked(ee, 28 * p, 14), picked(ee, 28 * p + 14, 14)], axis=1)

    acc = jnp.zeros((HALF, 256), F32)
    for p in range(9):
        rhs = jnp.concatenate([dcw[0, :, 256 * p : 256 * p + 256], dcw[1, :, 256 * p : 256 * p + 256]], axis=0)
        acc = acc + dot(err_cols(p), rhs, 1, 1)
    tw = l1_coeff * twb[pl.ds(off, HALF)]
    acc = acc + jnp.concatenate([tw, tw], axis=1)
    pg = jnp.where(pa[...] > 0.0, acc, 0.0).astype(BF16)
    for p in range(9):
        r = dot(st[256 * p : 256 * p + 256, 0:HALF], pg)
        eg[256 * p : 256 * p + 256] = r[:, 0:128]
        egs[256 * p : 256 * p + 256] = r[:, 128:256].astype(BF16)
        if p % 3 == 2:
            part = pl.ds(768 * (p // 3), 768)
            send(egs.at[part], egr.at[part], 13, other, 44 + p // 3)
    lt = lat_t[:, 0:HALF]
    for p in range(9):
        r = dot(lt, err_cols(p))
        dg[:, 256 * p : 256 * p + 256] = r[0:128]
        dgs[:, 256 * p : 256 * p + 256] = r[128:256].astype(BF16)
        if p % 3 == 2:
            part = pl.ds(768 * (p // 3), 768)
            send(dgs.at[:, part], dgr.at[:, part], 14, other, 47 + p // 3)
    acc = jnp.zeros((8, 128), F32)
    for p in range(18):
        if p % 6 == 0:
            arrived(egr.at[0:768], 44 + p // 6)
        v = eg[128 * p : 128 * p + 128] + egr[128 * p : 128 * p + 128].astype(F32)
        eg[128 * p : 128 * p + 128] = v
        acc = acc + jnp.sum((v * v).reshape(16, 8, 128), axis=0)
    for p in range(18):
        if p % 6 == 0:
            arrived(dgr.at[:, 0:768], 47 + p // 6)
        v = dg[:, 128 * p : 128 * p + 128] + dgr[:, 128 * p : 128 * p + 128].astype(F32)
        dg[:, 128 * p : 128 * p + 128] = v
        acc = acc + jnp.sum((v * v).reshape(16, 8, 128), axis=0)

    n7[0] = acc

    def send_n(d):
        k = far_first(ZN, d)
        send(n7.at[0], n7z.at[k - 1], 15, z_peer(k), 50)

    loop(ZN, send_n)

    left(p1r, 0)
    left(sqr, 1)

    @pl.when(c == half)
    def _():
        left(hh.at[0, 0:28], 2)
        left(hh.at[1, 0:28], 2)

    @pl.when(c != half)
    def _():
        left(hh, 2)

    left(p3r, 3)
    gathered(gs, 17)
    left(p5r.at[:, 0:12], 7)
    left(zb, 8)
    left(p5z, 9)
    gathered(ee, 22)
    left(egs, 13)
    left(dgs, 14)
    for k in range(3, 7):
        loads[k].wait()
    arrived(n7z, 50)
    for d in range(15):
        acc = acc + n7z[d]
    n7[1] = acc

    def send_xy(d):
        send(n7.at[1], n7x.at[d - 1], 16, xy_peer(d), 51)
        send(n7.at[1], n7x.at[d + 15], 16, xy_peer(d, 1 - c), 51)

    loop(16, send_xy)
    send(n7.at[1], n7x.at[15], 16, other, 51)
    arrived(n7x, 51)
    for d in range(31):
        acc = acc + n7x[d]
    clip[...] = jnp.broadcast_to(lax.rsqrt(jnp.sum(acc, keepdims=True) + 1e-12), (8, 128))

    left(n7z, 15)
    left(n7x, 16)


def local(
    residual, token_ids, ffn_gain, gate_w, up_w, down_w, enc_w, enc_bias, dec_w, dec_bias,
    enc_first, enc_second, dec_first, dec_second,
):
    vm = pl.BlockSpec(memory_space=pltpu.VMEM)
    hbm = pl.BlockSpec(memory_space=pl.ANY)
    V = pltpu.VMEM
    scratch = [
        V((W, TOK), BF16), V((W,), BF16), V((W, W), BF16), V((W, W), BF16), V((1, TOK), jnp.int32),
        V((1, 128), BF16), V((D,), BF16), V((W, W), BF16), V((2, D, 128), BF16), V((2, 128, D), BF16), V((2, 8, 128), F32),
        V((512, W), BF16), V((512, 128), F32), V((64, 16, 128), F32), V((2, 64, 16, 128), BF16),
        V((7, 2, 8, 16, 128), BF16), V((8, 128), F32), V((7, 8, 128), F32), V((8, 16, 128), BF16),
        V((2, 32, 16, 128), BF16), V((2, 384, 384), BF16), V((512, 256), F32), V((32, 16, 128), F32),
        V((32, 16, 128), BF16), V((31, 16, 128), BF16),
        V((4, 4, 16, 16, 128), BF16), V((256, 16, 128), BF16), V((512, 128), F32), V((18, 8, 128), F32),
        V((HALF, 256), F32), V((256, 256), BF16), V((16, 16, 16, 128), BF16), V((15, 16, 16, 128), BF16),
        V((4, 16, 16, 128), BF16), V((16, 16, 128), BF16), V((16, 16, 128), BF16), V((11, 16, 128), BF16),
        V((4, 4, 16, 16, 128), BF16), V((D, 256), BF16),
        V((128, D), BF16), V((128, D), BF16), V((D, 128), BF16), V((D, 128), BF16),
        V((2, 8, 128), F32), V((15, 8, 128), F32), V((31, 8, 128), F32),
        pltpu.SemaphoreType.DMA((14,)), pltpu.SemaphoreType.DMA((4,)), pltpu.SemaphoreType.DMA((4,)),
        pltpu.SemaphoreType.DMA((27,)), pltpu.SemaphoreType.DMA((83,)),
    ]
    operands = [
        pltpu.with_memory_space_constraint(v, pltpu.HBM)
        for v in (
            residual.T, token_ids.reshape(1, TOK), ffn_gain, gate_w, up_w, down_w, enc_w,
            enc_bias.reshape(1, 128), dec_w, dec_bias, enc_first, enc_second, dec_first, dec_second,
        )
    ]
    tall, flat = jax.ShapeDtypeStruct((D, 128), BF16), jax.ShapeDtypeStruct((128, D), BF16)
    enc_grad, dec_grad, clip, enc_one, enc_two, dec_one, dec_two = pl.pallas_call(
        kernel,
        out_shape=(
            jax.ShapeDtypeStruct((D, 128), F32),
            jax.ShapeDtypeStruct((128, D), F32),
            jax.ShapeDtypeStruct((8, 128), F32),
            tall, tall, flat, flat,
        ),
        in_specs=[hbm] * 14,
        out_specs=(vm,) * 7,
        scratch_shapes=scratch,
        compiler_params=pltpu.CompilerParams(
            collective_id=0, has_side_effects=True, vmem_limit_bytes=32 << 20
        ),
    )(*operands)
    return pl.pallas_call(
        adam_kernel,
        out_shape=(tall, flat),
        in_specs=[vm] * 7,
        out_specs=(hbm, hbm),
        scratch_shapes=[V((D, 128), BF16), V((128, D), BF16), pltpu.SemaphoreType.DMA((12,))],
        compiler_params=pltpu.CompilerParams(vmem_limit_bytes=16 << 20),
    )(clip, enc_grad, enc_one, enc_two, dec_grad, dec_one, dec_two)


def solution(mesh):
    in_specs = (
        P(None, "src"),
        P(),
        P("src"),
        P("src", "feat"),
        P("src", "feat"),
        P("feat", "src"),
        P(None, ("src", "feat")),
        P(("src", "feat")),
        P(("src", "feat"), None),
        P(),
        P(None, ("src", "feat")),
        P(None, ("src", "feat")),
        P(("src", "feat"), None),
        P(("src", "feat"), None),
    )
    out_specs = (P(None, ("src", "feat")), P(("src", "feat"), None))
    return jax.shard_map(local, mesh=mesh, in_specs=in_specs, out_specs=out_specs, check_vma=False)
```

```python
import functools

import jax
import jax.numpy as jnp
from jax import lax
from jax.experimental import pallas as pl
from jax.experimental.pallas import tpu as pltpu
from jax.sharding import PartitionSpec as P

SPECIAL = 4
TOK = 448
HALF = 224
D = 2304
W = 288
ZN = 16
SRC = 8
FEAT = 64

eps_rms = 1e-06
beta_one = 0.9
beta_two = 0.999
adam_count = 100.0
l1_coeff = 0.2

F32 = jnp.float32
BF16 = jnp.bfloat16


def tiles(v):
    return v.reshape(v.shape[0] // 16, 16, 128)


def rows(v):
    return v.reshape(v.shape[0] * 16, 128)


def dot(a, b, ca=1, cb=0):
    return lax.dot_general(a, b, (((ca,), (cb,)), ((), ())), preferred_element_type=F32)


def lane_group(shape):
    return lax.broadcasted_iota(jnp.int32, shape, len(shape) - 1)


def fold(read, lanes):
    out = read(3)
    for g in (2, 1, 0):
        out = jnp.where(lanes < 32 * (g + 1), read(g), out)
    return out


FAR = (8, 9, 7, 10, 6, 11, 5, 12, 4, 13, 3)
GROUPS = ((3, 5), (12, 14), (5, 7), (10, 12), (7, 8), (9, 10), (8, 9))
GROUP_OF = {place: g for g, (lo, hi) in enumerate(GROUPS) for place in range(lo, hi)}


def adam(grad, first, second, clip):
    corr_one = 1.0 - beta_one**adam_count
    corr_two = 1.0 - beta_two**adam_count
    scaled_grad = clip * grad
    mean = (beta_one / corr_one) * first.astype(F32) + ((1.0 - beta_one) / corr_one) * scaled_grad
    power = (beta_two / corr_two) * second.astype(F32) + ((1.0 - beta_two) / corr_two) * (scaled_grad * scaled_grad)
    return (mean / (jnp.sqrt(power) + 1e-08)).astype(BF16)


def adam_kernel(clip, eg, ef, es, dg, df, ds, eo_h, do_h, eo, do, sem):
    scale = clip[0:1, 0:1]
    copies = []
    for p in range(6):
        at = slice(384 * p, 384 * p + 384)
        do[:, at] = adam(dg[:, at], df[:, at], ds[:, at], scale)
        copies.append(pltpu.make_async_copy(do.at[:, at], do_h.at[:, at], sem.at[2 * p]))
        copies[-1].start()
        eo[at] = adam(eg[at], ef[at], es[at], scale)
        copies.append(pltpu.make_async_copy(eo.at[at], eo_h.at[at], sem.at[2 * p + 1]))
        copies[-1].start()
    for cp in copies:
        cp.wait()


def kernel(
    res_h, tok_h, gain_h, gw_h, uw_h, dw_h, ew_h, eb_h, dcw_h, db_h, ef_h, es_h, df_h, ds_h,
    eg, dg, clip, ef, es, df, ds,
    res_t, gain, gw, uw, tok, eb, db, dw, ew, dcw, ebx,
    rf, rn, rt, gu, p1r, sqs, sqr, hb, hh, dwf, tail, rest, ot, p3r,
    gs, ss, twb, bias, pa, lat_t, tt, p5r, zb, own, aa, p5z, ee, st,
    dgs, dgr, egs, egr, n7, n7z, n7x,
    lsem, wsend, wrecv, ssem, rsem,
):
    s = lax.axis_index("src")
    f = lax.axis_index("feat")
    c = lax.rem(f, 2)
    q = lax.div(f, 2)
    z = lax.rem(q, ZN)
    yhi = lax.div(q, ZN)
    xy = s * 2 + yhi
    half = lax.div(s, 4)
    x = lax.div(s, 2)
    y = lax.rem(s, 2) * 2 + yhi

    def to(src, feat):
        return {"device_id": (src, feat), "device_id_type": pl.DeviceIdType.MESH}

    other = to(s, q * 2 + 1 - c)

    def src_peer(d, core):
        return to(lax.rem(s + d, SRC), q * 2 + core)

    def q_peer(d):
        return to(s, lax.rem(q + d, 32) * 2 + c)

    def z_peer(d):
        return to(s, (yhi * ZN + lax.rem(z + d, ZN)) * 2 + c)

    def xy_index(d):
        return lax.rem(x + lax.div(d, 4), 4) * 4 + lax.rem(y + lax.rem(d, 4), 4)

    def xy_peer(d, core=c):
        i = xy_index(d)
        return to(lax.div(i, 2), (lax.rem(i, 2) * ZN + z) * 2 + core)

    def x_peer(d):
        return to(lax.rem(x + d, 4) * 2 + lax.div(y, 2), f)

    def y_peer(d):
        k = lax.rem(y + d, 4)
        return to(x * 2 + lax.div(k, 2), (lax.rem(k, 2) * ZN + z) * 2 + c)

    def loop(n, fn):
        def body(d, carry):
            fn(d)
            return carry

        lax.fori_loop(1, n, body, 0)

    def loop_xy(fn):
        loop(16, lambda d: fn(lax.rem(26 - d, 15) + 1))

    def send(src, dst, k, where, at=None):
        pltpu.make_async_remote_copy(
            src_ref=src, dst_ref=dst, send_sem=ssem.at[k], recv_sem=rsem.at[k if at is None else at], **where
        ).start()

    def arrived(ref, k):
        pltpu.make_async_copy(ref, ref, rsem.at[k]).wait()

    def left(ref, k):
        pltpu.make_async_copy(ref, ref, ssem.at[k]).wait()

    place_of = [lax.rem(k + ZN - z, ZN) for k in range(ZN)]

    def far_first(n, d):
        step = lax.div(d, 2)
        return n // 2 + jnp.where(lax.rem(d, 2) == 0, step, -step)

    def gather(buf, k, m):
        mine = buf.at[x, y, 0]
        for d in FAR:
            send(mine, buf.at[x, y, ZN - d], k, z_peer(d), m + GROUP_OF[ZN - d])
        loop_xy(lambda d: send(mine, mine, k + 1, xy_peer(d), m + 7))

        def first(g):
            lo, hi = GROUPS[g]
            arrived(buf.at[0, 0, lo:hi], m + g)
            part = buf.at[x, y, lo:hi]
            for d in (2, 1, 3):
                send(part, part, k + 3, x_peer(d) if g % 2 == 0 else y_peer(d), m + 10 + g)

        def second(g):
            lo, hi = GROUPS[g]
            arrived(buf.at[0:3, 0, lo:hi], m + 10 + g)
            part = buf.at[:, y, lo:hi] if g % 2 == 0 else buf.at[x, :, lo:hi]
            for d in (2, 1, 3):
                send(part, part, k + 4, y_peer(d) if g % 2 == 0 else x_peer(d), m + 14)

        def direct(g):
            lo, hi = GROUPS[g]
            arrived(buf.at[0, 0, lo:hi], m + g)
            part = buf.at[x, y, lo:hi]
            loop_xy(lambda d: send(part, part, k + 1, xy_peer(d), m + 8))

        first(0)
        first(1)
        arrived(buf.at[0, 0, 0:15], m + 7)
        for d in (2, 14, 1, 15):
            send(buf.at[:, :, 0], buf.at[:, :, ZN - d], k + 2, z_peer(d), m + 9)
        first(2)
        first(3)
        for g in (4, 5, 6):
            direct(g)
        for g in (0, 1, 2, 3):
            second(g)
        arrived(buf.at[0:3, 0:3, 0:5], m + 8)
        arrived(buf.at[0:3, :, 0:8], m + 14)
        arrived(buf.at[:, :, 0:4], m + 9)

    def gathered(buf, k):
        left(buf.at[0, 0, 0:11], k)
        left(buf.at[0:3, :, 0:5], k + 1)
        left(buf.at[:, :, 0:4], k + 2)
        left(buf.at[0:3, 0, 0:8], k + 3)
        left(buf.at[0:3, :, 0:8], k + 4)

    fetched = []
    for k, (src, dst) in enumerate(((res_h, res_t), (gain_h, gain), (gw_h, gw), (uw_h, uw), (tok_h, tok), (eb_h, eb), (db_h, db))):
        cp = pltpu.make_async_copy(src, dst, lsem.at[7 + k])
        cp.start()
        fetched.append(cp)

    barrier = pltpu.get_barrier_semaphore()

    def greet(where):
        pl.semaphore_signal(barrier, inc=1, **where)

    def greet_z(d):
        k = far_first(ZN, d)
        greet(q_peer(k))
        greet(q_peer(k + 16))

    def greet_src(d):
        k = far_first(SRC, d)
        greet(src_peer(k, c))
        greet(src_peer(k, 1 - c))
        for core in (c, 1 - c):
            greet(to(lax.rem(s + k, SRC), (lax.rem(yhi + 1, 2) * ZN + z) * 2 + core))

    loop(ZN, greet_z)
    loop(SRC, greet_src)
    greet(q_peer(16))
    greet(other)
    greet(to(s, (lax.rem(yhi + 1, 2) * ZN + z) * 2 + 1 - c))

    loads = []
    for k, (src, dst) in enumerate(
        ((dw_h, dw), (ew_h, ew.at[0]), (dcw_h, dcw.at[0]), (ef_h, ef), (es_h, es), (df_h, df), (ds_h, ds))
    ):
        cp = pltpu.make_async_copy(src, dst, lsem.at[k])
        cp.start()
        loads.append(cp)

    lanes = lane_group((64, 128))
    pick = jnp.where(
        jnp.bitwise_and(lane_group((32, 128)), 31) == lax.broadcasted_iota(jnp.int32, (32, 128), 0), 1.0, 0.0
    ).astype(BF16)

    tail[448:512] = jnp.zeros((64, 256), F32)
    fetched[0].wait()
    fetched[1].wait()
    rf[...] = jnp.concatenate([res_t[...], jnp.zeros((W, 64), BF16)], axis=1).T
    xg = (rf[0:448].astype(F32) * gain[...].astype(F32).reshape(1, W)).astype(BF16)
    fetched[2].wait()
    fetched[3].wait()
    spread = dot(jnp.concatenate([gw[:, 256:288], uw[:, 256:288]], axis=0), pick).astype(BF16)
    tail[0:448] = dot(xg, jnp.concatenate([spread[0:W], spread[W : 2 * W]], axis=1))
    for k, w in enumerate((gw, uw)):
        main = dot(xg, w[:, 0:256])
        for h in range(2):
            for j in range(2):
                gu[k, h * 32 + 14 * j : h * 32 + 14 * j + 14] = tiles(
                    main[224 * h : 224 * h + 224, 128 * j : 128 * j + 128].astype(BF16)
                )
            part = fold(
                lambda g: tail[224 * h + 64 * g : 224 * h + 64 * g + 64, 128 * k : 128 * k + 128], lanes
            )
            gu[k, h * 32 + 28 : h * 32 + 32] = tiles(part.astype(BF16))
    wide = res_t[...].astype(F32)
    squares = jnp.sum(wide * wide, axis=0, keepdims=True)
    squares = jnp.concatenate([squares, jnp.zeros((1, 64), F32)], axis=1)
    sqs[...] = jnp.concatenate(
        [squares[:, 128 * k : 128 * k + 128] for k in range(4)] + [jnp.zeros((4, 128), F32)], axis=0
    )

    pl.semaphore_wait(barrier, 61)

    def send_p1(d):
        k = far_first(SRC, d)
        send(sqs, sqr.at[k - 1], 1, src_peer(k, c))
        send(gu.at[:, pl.ds(8 * lax.rem(s + k, SRC), 4)], p1r.at[k - 1, :, 0:4], 0, src_peer(k, c))

    def send_p1_rest(d):
        k = far_first(SRC, d)
        send(gu.at[:, pl.ds(8 * lax.rem(s + k, SRC) + 4, 4)], p1r.at[k - 1, :, 4:8], 0, src_peer(k, c), 82)

    loop(SRC, send_p1)
    loop(SRC, send_p1_rest)

    for k in (4, 5, 6):
        fetched[k].wait()
    ids = tok[...]
    live = jnp.where(ids >= SPECIAL, 1.0, 0.0)
    weight = live / jnp.maximum(jnp.sum(live), 1.0)
    weight = jnp.concatenate([weight, jnp.zeros((1, 64), F32)], axis=1)
    weight = jnp.concatenate(
        [weight[:, 128 * k : 128 * k + 128] for k in range(4)] + [jnp.zeros((124, 128), F32)], axis=0
    ).T
    for k in range(4):
        twb[128 * k : 128 * k + 128] = jnp.broadcast_to(weight[:, k : k + 1], (128, 128))
    for k in range(18):
        bias[k] = jnp.broadcast_to(db[128 * k : 128 * k + 128].astype(F32).reshape(1, 128), (8, 128))
    ebx[0] = jnp.broadcast_to(eb[...].astype(F32), (8, 128))

    def share(ref, k):
        return pltpu.make_async_remote_copy(
            src_ref=ref.at[0], dst_ref=ref.at[1], send_sem=wsend.at[k], recv_sem=wrecv.at[k], **other
        )

    shares = [share(ebx, 0), share(dwf, 1), share(ew, 2), share(dcw, 3)]
    shares[0].start()
    loads[0].wait()
    spread = dot(dw[:, 256:288], pick).astype(BF16)
    dwf[0, 0:256, 0:256] = dw[0:256, 0:256]
    dwf[0, 0:256, 256:384] = spread[0:256]
    for g in range(4):
        dwf[0, 256 + 32 * g : 288 + 32 * g, 0:256] = dw[256:288, 0:256]
        dwf[0, 256 + 32 * g : 288 + 32 * g, 256:384] = spread[256:288]
    shares[1].start()
    loads[1].wait()
    shares[2].start()
    loads[2].wait()
    shares[3].start()

    off = pl.multiple_of(HALF * c, 32)
    for j in range(2):
        rest[14 * j : 14 * j + 14] = tiles(rf[pl.ds(off, HALF), 128 * j : 128 * j + 128].astype(F32))
    tail[:, 0:128] = dot(rf[:, 256:288], pick)
    rest[28:32] = tiles(fold(lambda g: tail[pl.ds(off + 64 * g, 64), 0:128], lanes))
    ss[252:256] = jnp.zeros((4, 16, 128), BF16)
    for k in range(12, 16):
        tt[15, place_of[k]] = jnp.zeros((16, 128), BF16)

    arrived(sqr, 1)
    total = sqs[...]
    for d in range(7):
        total = total + sqr[d]
    inv = lax.rsqrt(total / D + eps_rms)
    inv = jnp.concatenate([inv, jnp.zeros((120, 128), F32)], axis=0).T
    for k in range(4):
        rn[128 * k : 128 * k + 128] = jnp.broadcast_to(inv[:, k : k + 1], (128, 128))
    for h in range(2):
        for j in range(2):
            rt[h * 32 + 14 * j : h * 32 + 14 * j + 14] = tiles(rn[224 * h : 224 * h + 224])
        rt[h * 32 + 28 : h * 32 + 32] = tiles(
            fold(lambda g: rn[224 * h + 64 * g : 224 * h + 64 * g + 64], lanes)
        )

    slot = jnp.where(c == half, 0, 1)
    for n in range(2):
        at = slice(4 * n, 4 * n + 4)
        arrived(p1r.at[:, :, at], 82 * n)
        acts = []
        for k in range(2):
            acc = gu[k, pl.ds(8 * s + 4 * n, 4)].astype(F32)
            for d in range(7):
                acc = acc + p1r[d, k, at].astype(F32)
            acts.append(acc * rt[pl.ds(8 * s + 4 * n, 4)])
        hb[at] = (jax.nn.gelu(acts[0], approximate=True) * acts[1]).astype(BF16)
        ours = hb.at[at]
        place = hh.at[slot, pl.ds(8 * lax.rem(s, 4) + 4 * n, 4)]

        @pl.when(c == half)
        def _():
            pltpu.make_async_copy(ours, place, rsem.at[2]).start()

        @pl.when(c != half)
        def _():
            send(ours, place, 2, src_peer(0, half))

        loop(SRC, lambda d: send(ours, place, 2, src_peer(d, half)))
    shares[1].wait()
    arrived(hh, 2)
    acc = jnp.zeros((HALF, 384), F32)
    for k in range(2):
        last = rows(hh[k, 28:32])
        keep = jnp.zeros_like(last)
        split = jnp.concatenate(
            [jnp.where((lanes >= 32 * g) & (lanes < 32 * g + 32), last, keep) for g in range(4)], axis=0
        )[0:HALF]
        lhs = jnp.concatenate([rows(hh[k, 0:14]), rows(hh[k, 14:28]), split], axis=1)
        acc = acc + dot(lhs, dwf[k])
    for j in range(2):
        ot[14 * j : 14 * j + 14] = tiles(acc[:, 128 * j : 128 * j + 128].astype(BF16))
    tail[0:224, 0:128] = acc[:, 256:384]
    ot[28:32] = tiles(fold(lambda g: tail[64 * g : 64 * g + 64, 0:128], lanes).astype(BF16))


    def send_p3(d):
        k = far_first(ZN, d)
        send(ot.at[lax.rem(q + k, 32)], p3r.at[k - 1], 3, q_peer(k))
        send(ot.at[lax.rem(q + k + 16, 32)], p3r.at[k + 15], 3, q_peer(k + 16))

    loop(ZN, send_p3)
    send(ot.at[lax.rem(q + 16, 32)], p3r.at[15], 3, q_peer(16))
    arrived(p3r, 3)
    acc = ot[q].astype(F32)
    for d in range(31):
        acc = acc + p3r[d].astype(F32)
    gs[x, y, 0] = (rest[q] + acc).astype(BF16)

    gather(gs, 17, 52)

    def picked(buf, first, n):
        return jnp.concatenate([buf[t // 64, t // 16 % 4, place_of[t % 16]] for t in range(first, first + n)], axis=0)

    acc = jnp.zeros((HALF, 128), F32)
    rem = jnp.zeros((64, 128), F32)
    for k in range(SRC):
        for j in range(2):
            v = picked(gs, 32 * k + 14 * j, 14).astype(F32)
            acc = acc + v * v
        v = picked(gs, 32 * k + 28, 4).astype(F32)
        rem = rem + v * v
    acc = acc + jnp.concatenate(
        [jnp.where((lanes >= 32 * g) & (lanes < 32 * g + 32), rem, 0.0) for g in range(4)], axis=0
    )[0:HALF]
    inv = lax.rsqrt(jnp.sum(acc, axis=1, keepdims=True) / D + eps_rms)
    tall = lane_group((HALF, 128))

    def turn(v, by):
        by = by % 128
        return v if by == 0 else pltpu.roll(v, by, 1)

    for k in range(SRC):
        m, base = k % 4, 9 * (k // 4)
        a0 = turn(picked(gs, 32 * k, 14).astype(F32) * inv, 32 * m)
        a1 = turn(picked(gs, 32 * k + 14, 14).astype(F32) * inv, 32 * m)
        last = picked(gs, 32 * k + 28, 4).astype(F32)
        rem = jnp.concatenate([turn(last, 32 * m - 32 * g) for g in range(4)], axis=0)[0:HALF] * inv
        if m == 0:
            first, second = a0, a1
        else:
            first = jnp.where(tall < 32 * m, carry, a0)
            second = jnp.where(tall < 32 * m, a0, a1)
        carry = jnp.where(tall < 32 * m, a1, rem)
        for at, v in ((2 * m, first), (2 * m + 1, second)) + (((8, carry),) if m == 3 else ()):
            ss[14 * (base + at) : 14 * (base + at) + 14] = tiles(v.astype(BF16))

    def cols_of(ref, p):
        return jnp.concatenate([rows(ref[28 * p : 28 * p + 14]), rows(ref[28 * p + 14 : 28 * p + 28])], axis=1)

    for k in (0, 2, 3):
        shares[k].wait()
    acc = jnp.zeros((HALF, 256), F32)
    for p in range(9):
        rhs = jnp.concatenate([ew[0, 256 * p : 256 * p + 256], ew[1, 256 * p : 256 * p + 256]], axis=1)
        acc = acc + dot(cols_of(ss, p), rhs)
    acc = acc + jnp.concatenate([ebx[0, 0:1], ebx[1, 0:1]], axis=1)
    pa[...] = acc
    latents = jnp.maximum(acc, 0.0)
    lat = latents.astype(BF16)
    for p in range(9):
        rhs = jnp.concatenate([dcw[0, :, 256 * p : 256 * p + 256], dcw[1, :, 256 * p : 256 * p + 256]], axis=0)
        r = dot(lat, rhs).astype(BF16)
        for t in range(28 * p, 28 * p + 28):
            k = t - 28 * p
            tt[t // 16, place_of[t % 16]] = r[16 * (k % 14) : 16 * (k % 14) + 16, 128 * (k // 14) : 128 * (k // 14) + 128]

    def across(g):
        lo, hi = GROUPS[g]
        loop_xy(
            lambda d: send(
                tt.at[xy_index(d), lo:hi], p5r.at[d - 1, lo:hi], 7, xy_peer(d), 24 + g
            ),
        )

    for k, d in enumerate((2, 14, 1, 15)):
        send(tt.at[:, d], zb.at[k], 8, z_peer(d), 31)
    for g in (6, 4, 5):
        across(g)
    for g in (2, 3, 0, 1):
        across(g)
    lat_t[...] = jnp.concatenate([latents, jnp.zeros((32, 256), F32)], axis=0).T.astype(BF16)
    for p in range(18):
        v = rows(ss[14 * p : 14 * p + 14]).astype(F32)
        st[128 * p : 128 * p + 128] = jnp.concatenate([v, jnp.zeros((32, 128), F32)], axis=0).T.astype(BF16)

    def onward(g):
        lo, hi = GROUPS[g]
        arrived(p5r.at[:, lo:hi], 24 + g)
        for k in range(lo, hi):
            acc = tt[xy, k].astype(F32)
            for d in range(15):
                acc = acc + p5r[d, k].astype(F32)
            aa[k] = acc.astype(BF16)
            send(aa.at[k], p5z.at[k - 3], 9, z_peer(k), 33)

    for g in (6, 4, 5):
        onward(g)
    arrived(zb, 31)
    for k in range(16):
        acc = tt[k, 0].astype(F32)
        for d in range(4):
            acc = acc + zb[d, k].astype(F32)
        own[k] = acc.astype(BF16)
    loop_xy(lambda d: send(own.at[xy_index(d)], p5r.at[d - 1, 0], 7, xy_peer(d), 32))
    for g in (2, 3, 0, 1):
        onward(g)
    arrived(p5r.at[:, 0], 32)
    acc = own[xy].astype(F32)
    for d in range(15):
        acc = acc + p5r[d, 0].astype(F32)
    arrived(p5z, 33)
    for d in range(11):
        acc = acc + p5z[d].astype(F32)
    t = xy * 16 + z
    col = jnp.minimum(lax.div(t, 14), 17)
    row = lax.rem(t, 14)
    err = (acc + bias[col, 0:1] - ss[t].astype(F32)).astype(BF16)
    tw = twb[pl.ds(pl.multiple_of(off + 16 * row, 16), 16)]
    ee[x, y, 0] = (2.0 * tw * err.astype(F32)).astype(BF16)
    gather(ee, 22, 67)

    def err_cols(p):
        return jnp.concatenate([picked(ee, 28 * p, 14), picked(ee, 28 * p + 14, 14)], axis=1)

    acc = jnp.zeros((HALF, 256), F32)
    for p in range(9):
        rhs = jnp.concatenate([dcw[0, :, 256 * p : 256 * p + 256], dcw[1, :, 256 * p : 256 * p + 256]], axis=0)
        acc = acc + dot(err_cols(p), rhs, 1, 1)
    tw = l1_coeff * twb[pl.ds(off, HALF)]
    acc = acc + jnp.concatenate([tw, tw], axis=1)
    pg = jnp.where(pa[...] > 0.0, acc, 0.0).astype(BF16)
    for p in range(9):
        r = dot(st[256 * p : 256 * p + 256, 0:HALF], pg)
        eg[256 * p : 256 * p + 256] = r[:, 0:128]
        egs[256 * p : 256 * p + 256] = r[:, 128:256].astype(BF16)
        if p % 3 == 2:
            part = pl.ds(768 * (p // 3), 768)
            send(egs.at[part], egr.at[part], 13, other, 44 + p // 3)
    lt = lat_t[:, 0:HALF]
    for p in range(9):
        r = dot(lt, err_cols(p))
        dg[:, 256 * p : 256 * p + 256] = r[0:128]
        dgs[:, 256 * p : 256 * p + 256] = r[128:256].astype(BF16)
        if p % 3 == 2:
            part = pl.ds(768 * (p // 3), 768)
            send(dgs.at[:, part], dgr.at[:, part], 14, other, 47 + p // 3)
    acc = jnp.zeros((8, 128), F32)
    for p in range(18):
        if p % 6 == 0:
            arrived(egr.at[0:768], 44 + p // 6)
        v = eg[128 * p : 128 * p + 128] + egr[128 * p : 128 * p + 128].astype(F32)
        eg[128 * p : 128 * p + 128] = v
        acc = acc + jnp.sum((v * v).reshape(16, 8, 128), axis=0)
    for p in range(18):
        if p % 6 == 0:
            arrived(dgr.at[:, 0:768], 47 + p // 6)
        v = dg[:, 128 * p : 128 * p + 128] + dgr[:, 128 * p : 128 * p + 128].astype(F32)
        dg[:, 128 * p : 128 * p + 128] = v
        acc = acc + jnp.sum((v * v).reshape(16, 8, 128), axis=0)

    n7[0] = acc

    def send_n(d):
        k = far_first(ZN, d)
        send(n7.at[0], n7z.at[k - 1], 15, z_peer(k), 50)

    loop(ZN, send_n)

    left(p1r, 0)
    left(sqr, 1)

    @pl.when(c == half)
    def _():
        left(hh.at[0, 0:28], 2)
        left(hh.at[1, 0:28], 2)

    @pl.when(c != half)
    def _():
        left(hh, 2)

    left(p3r, 3)
    gathered(gs, 17)
    left(p5r.at[:, 0:12], 7)
    left(zb, 8)
    left(p5z, 9)
    gathered(ee, 22)
    left(egs, 13)
    left(dgs, 14)
    for k in range(3, 7):
        loads[k].wait()
    arrived(n7z, 50)
    for d in range(15):
        acc = acc + n7z[d]
    n7[1] = acc

    def send_xy(d):
        send(n7.at[1], n7x.at[d - 1], 16, xy_peer(d), 51)
        send(n7.at[1], n7x.at[d + 15], 16, xy_peer(d, 1 - c), 51)

    loop_xy(send_xy)
    send(n7.at[1], n7x.at[15], 16, other, 51)
    arrived(n7x, 51)
    for d in range(31):
        acc = acc + n7x[d]
    clip[...] = jnp.broadcast_to(lax.rsqrt(jnp.sum(acc, keepdims=True) + 1e-12), (8, 128))

    left(n7z, 15)
    left(n7x, 16)


def local(
    residual, token_ids, ffn_gain, gate_w, up_w, down_w, enc_w, enc_bias, dec_w, dec_bias,
    enc_first, enc_second, dec_first, dec_second,
):
    vm = pl.BlockSpec(memory_space=pltpu.VMEM)
    hbm = pl.BlockSpec(memory_space=pl.ANY)
    V = pltpu.VMEM
    scratch = [
        V((W, TOK), BF16), V((W,), BF16), V((W, W), BF16), V((W, W), BF16), V((1, TOK), jnp.int32),
        V((1, 128), BF16), V((D,), BF16), V((W, W), BF16), V((2, D, 128), BF16), V((2, 128, D), BF16), V((2, 8, 128), F32),
        V((512, W), BF16), V((512, 128), F32), V((64, 16, 128), F32), V((2, 64, 16, 128), BF16),
        V((7, 2, 8, 16, 128), BF16), V((8, 128), F32), V((7, 8, 128), F32), V((8, 16, 128), BF16),
        V((2, 32, 16, 128), BF16), V((2, 384, 384), BF16), V((512, 256), F32), V((32, 16, 128), F32),
        V((32, 16, 128), BF16), V((31, 16, 128), BF16),
        V((4, 4, 16, 16, 128), BF16), V((256, 16, 128), BF16), V((512, 128), F32), V((18, 8, 128), F32),
        V((HALF, 256), F32), V((256, 256), BF16), V((16, 16, 16, 128), BF16), V((15, 16, 16, 128), BF16),
        V((4, 16, 16, 128), BF16), V((16, 16, 128), BF16), V((16, 16, 128), BF16), V((11, 16, 128), BF16),
        V((4, 4, 16, 16, 128), BF16), V((D, 256), BF16),
        V((128, D), BF16), V((128, D), BF16), V((D, 128), BF16), V((D, 128), BF16),
        V((2, 8, 128), F32), V((15, 8, 128), F32), V((31, 8, 128), F32),
        pltpu.SemaphoreType.DMA((14,)), pltpu.SemaphoreType.DMA((4,)), pltpu.SemaphoreType.DMA((4,)),
        pltpu.SemaphoreType.DMA((27,)), pltpu.SemaphoreType.DMA((83,)),
    ]
    operands = [
        pltpu.with_memory_space_constraint(v, pltpu.HBM)
        for v in (
            residual.T, token_ids.reshape(1, TOK), ffn_gain, gate_w, up_w, down_w, enc_w,
            enc_bias.reshape(1, 128), dec_w, dec_bias, enc_first, enc_second, dec_first, dec_second,
        )
    ]
    tall, flat = jax.ShapeDtypeStruct((D, 128), BF16), jax.ShapeDtypeStruct((128, D), BF16)
    enc_grad, dec_grad, clip, enc_one, enc_two, dec_one, dec_two = pl.pallas_call(
        kernel,
        out_shape=(
            jax.ShapeDtypeStruct((D, 128), F32),
            jax.ShapeDtypeStruct((128, D), F32),
            jax.ShapeDtypeStruct((8, 128), F32),
            tall, tall, flat, flat,
        ),
        in_specs=[hbm] * 14,
        out_specs=(vm,) * 7,
        scratch_shapes=scratch,
        compiler_params=pltpu.CompilerParams(
            collective_id=0, has_side_effects=True, vmem_limit_bytes=32 << 20
        ),
    )(*operands)
    return pl.pallas_call(
        adam_kernel,
        out_shape=(tall, flat),
        in_specs=[vm] * 7,
        out_specs=(hbm, hbm),
        scratch_shapes=[V((D, 128), BF16), V((128, D), BF16), pltpu.SemaphoreType.DMA((12,))],
        compiler_params=pltpu.CompilerParams(vmem_limit_bytes=16 << 20),
    )(clip, enc_grad, enc_one, enc_two, dec_grad, dec_one, dec_two)


def solution(mesh):
    in_specs = (
        P(None, "src"),
        P(),
        P("src"),
        P("src", "feat"),
        P("src", "feat"),
        P("feat", "src"),
        P(None, ("src", "feat")),
        P(("src", "feat")),
        P(("src", "feat"), None),
        P(),
        P(None, ("src", "feat")),
        P(None, ("src", "feat")),
        P(("src", "feat"), None),
        P(("src", "feat"), None),
    )
    out_specs = (P(None, ("src", "feat")), P(("src", "feat"), None))
    return jax.shard_map(local, mesh=mesh, in_specs=in_specs, out_specs=out_specs, check_vma=False)
```
